512 devices in a mesh: stream: 16 (over z_hi, x), span: 32 (over z_lo, y, core).
Axes of the slice: x: 4, y: 8, z: 8 (z_hi: 4, z_lo: 2; z = z_hi * 2 + z_lo), core: 2. Of those that a mesh axis runs over, the one named last changes fastest.
Arguments:
- fine_pops: float32 [27, 96, 192, 128], P(None, 'stream', 'span'), may hold values from 0.5 to 2
- coarse_pops: float32 [27, 48, 96, 64], P(None, 'stream', 'span'), may hold values from 0.5 to 2
- obstacle: int32 [96, 192, 128], P('stream', 'span'), may hold values from 0 to 1, as said below
- block_level: int32 [16, 32], replicated, may hold values 0 or 1
- relax_rates: float32 [27], replicated, may hold values from 0.5 to 1.9
Outputs:
- fine_next: float32 [27, 96, 192, 128], P(None, 'stream', 'span')
- coarse_next: float32 [27, 48, 96, 64], P(None, 'stream', 'span')
The draws below stay inside these ranges and needn't reach their ends.
Inputs may be any that keep to these rules, and one draw needn't show every extreme that they name: `block_level`: 1 marks a refined block, whose fine cells are active; 0 a coarse block. `obstacle`: 1 marks a building cell. No building cell has a first index x with x % 6 below 2 or at least 4, nor a second index y with y % 6 below 2 or at least 4; a building cell stands on the ground or on another building cell.
All inputs are finite; a program needn't handle non-finite values.
Results may differ from the reference program's by a relative error of at most 0.0003.
Values sent between devices are 32-bit elements; how exact they have to be, the bound alone decides.
A program may use at most 64 MiB of HBM per device.

```python
import math
import jax
import jax.numpy as jnp
from jax import lax

BX = 6
BY = 6
BZ = 128
NX = 96
NY = 192
N_STREAM = 16
N_SPAN = 32


def draw_obstacle(key, part):
    heights = jax.random.randint(key, (NX, NY), -(BZ // 4), BZ // 2)
    heights = jnp.maximum(heights, 0)
    place_x = jnp.arange(NX) % BX
    place_y = jnp.arange(NY) % BY
    inner_x = (place_x >= 2) & (place_x < BX - 2)
    inner_y = (place_y >= 2) & (place_y < BY - 2)
    heights = jnp.where(inner_x[:, None] & inner_y[None, :], heights, 0)
    levels = jnp.arange(BZ)
    return (levels[None, None, :] < heights[:, :, None]).astype(jnp.int32)


def touch_ends(array, rng, smallest, high):
    dims = array.shape
    spot = [jax.random.randint(jax.random.fold_in(rng, axis), (), 0, dims[axis]) for axis in range(len(dims))]
    array = array.at[tuple(spot)].set(smallest)
    longest = dims.index(max(dims))
    spot[longest] = (spot[longest] + 1) % dims[longest]
    return array.at[tuple(spot)].set(high)


def block_levels(stream_key, extent, shards, smallest, top_value):
    factor_of, own = 1.0, jax.random.fold_in(stream_key, 6)
    for axis_at, blocks in shards:
        draws = jnp.exp(jax.random.uniform(jax.random.fold_in(own, axis_at), (blocks,), jnp.float32, smallest / len(shards), top_value / len(shards)))
        factor_of = factor_of * jnp.repeat(draws, extent[axis_at] // blocks).reshape([-1 if axis == axis_at else 1 for axis in range(len(extent))])
    return factor_of


def setup_inputs(seed: int = 0) -> dict:
    key_of = jax.random.split(jax.random.key(seed), 6)
    fine_pops = jnp.clip(jnp.exp(math.log(2.0) - 1.3862944 * jax.random.uniform(key_of[0], (27, NX, NY, BZ), jnp.float32) ** block_levels(key_of[0], (27, NX, NY, BZ), ((1, 16), (2, 32)), -0.2, 0.2)), 0.5, 2.0)
    coarse_pops = jnp.clip(jnp.exp(math.log(2.0) - 1.3862944 * jax.random.uniform(key_of[1], (27, NX // 2, NY // 2, BZ // 2), jnp.float32) ** block_levels(key_of[1], (27, NX // 2, NY // 2, BZ // 2), ((1, 16), (2, 32)), -0.2, 0.2)), 0.5, 2.0)
    obstacle = draw_obstacle(jax.random.fold_in(key_of[5], 71), 0)
    block_level = touch_ends((jax.random.randint(key_of[3], (N_STREAM, N_SPAN), 0, 2) < 1).astype(jnp.int32), jax.random.fold_in(key_of[3], 1), 0, 1)
    relax_rates = jnp.clip(jax.random.uniform(key_of[4], (27,), jnp.float32, 0.5, 1.9), 0.5, 1.9)
    return {"fine_pops": fine_pops, "coarse_pops": coarse_pops, "obstacle": obstacle, "block_level": block_level, "relax_rates": relax_rates}


def weight_table():
    single = jnp.where(jnp.arange(3) == 1, 2.0 / 3.0, 1.0 / 6.0).astype(jnp.float32)
    return single[:, None, None] * single[None, :, None] * single[None, None, :]


def central(moments, velocity, axis):
    minus_part = lax.index_in_dim(moments, 0, axis, False)
    zero_part = lax.index_in_dim(moments, 1, axis, False)
    plus_part = lax.index_in_dim(moments, 2, axis, False)
    summed = minus_part + zero_part + plus_part
    difference = plus_part - minus_part
    sum_pair = plus_part + minus_part
    first_order = difference - velocity * summed
    second = sum_pair - 2.0 * velocity * difference + velocity * velocity * summed
    return jnp.stack([summed, first_order, second], axis=axis)


def restore(moments, velocity, axis):
    zeroth = lax.index_in_dim(moments, 0, axis, False)
    first_order = lax.index_in_dim(moments, 1, axis, False)
    second = lax.index_in_dim(moments, 2, axis, False)
    square = velocity * velocity
    zero_part = zeroth * (1.0 - square) - 2.0 * velocity * first_order - second
    plus_part = 0.5 * (second + (2.0 * velocity + 1.0) * first_order + (square + velocity) * zeroth)
    minus_part = 0.5 * (second + (2.0 * velocity - 1.0) * first_order + (square - velocity) * zeroth)
    return jnp.stack([minus_part, zero_part, plus_part], axis=axis)


def collide(scaled, rates):
    others = scaled.shape[1:]
    table = weight_table().reshape(3, 3, 3, 1, 1, 1)
    pops = scaled.reshape((3, 3, 3) + others) * table
    density = jnp.sum(pops, axis=(0, 1, 2))
    velocity_x = jnp.sum(pops[2] - pops[0], axis=(0, 1)) / density
    velocity_y = jnp.sum(pops[:, 2] - pops[:, 0], axis=(0, 1)) / density
    velocity_z = jnp.sum(pops[:, :, 2] - pops[:, :, 0], axis=(0, 1)) / density
    moments = central(pops, velocity_x, 0)
    moments = central(moments, velocity_y, 1)
    moments = central(moments, velocity_z, 2)
    single = jnp.where(jnp.arange(3) == 0, 1.0, jnp.where(jnp.arange(3) == 1, 0.0, 1.0 / 3.0)).astype(jnp.float32)
    target = (single[:, None, None] * single[None, :, None] * single[None, None, :]).reshape(3, 3, 3, 1, 1, 1) * density
    moments = moments - rates.reshape(3, 3, 3, 1, 1, 1) * (moments - target)
    moments = restore(moments, velocity_z, 2)
    moments = restore(moments, velocity_y, 1)
    moments = restore(moments, velocity_x, 0)
    return (moments / table).reshape((27,) + others)


def shift_height(source, bounce, step):
    if step == 0:
        return source, bounce
    edge_value = jnp.zeros_like(source[..., :1])
    edge_bounce = jnp.ones_like(bounce[..., :1])
    if step == 1:
        return (jnp.concatenate([edge_value, source[..., :-1]], axis=-1),
                jnp.concatenate([edge_bounce, bounce[..., :-1]], axis=-1))
    return (jnp.concatenate([source[..., 1:], edge_value], axis=-1),
            jnp.concatenate([bounce[..., 1:], edge_bounce], axis=-1))


def stream_pull(padded, blocked):
    size_x = padded.shape[1] - 2
    size_y = padded.shape[2] - 2
    center = padded[:, 1:-1, 1:-1]
    pieces = []
    for pop_index in range(27):
        step_x = pop_index // 9 - 1
        step_y = pop_index // 3 % 3 - 1
        step_z = pop_index % 3 - 1
        source = padded[pop_index, 1 - step_x:1 - step_x + size_x, 1 - step_y:1 - step_y + size_y]
        bounce = blocked[1 - step_x:1 - step_x + size_x, 1 - step_y:1 - step_y + size_y]
        source, bounce = shift_height(source, bounce, step_z)
        pieces.append(jnp.where(bounce, center[26 - pop_index], source))
    return jnp.stack(pieces)


def refine_axis(values, axis):
    length = values.shape[axis]
    middle = lax.slice_in_dim(values, 1, length - 1, axis=axis)
    before = lax.slice_in_dim(values, 0, length - 2, axis=axis)
    after = lax.slice_in_dim(values, 2, length, axis=axis)
    lower = 0.75 * middle + 0.25 * before
    higher = 0.75 * middle + 0.25 * after
    shape = list(middle.shape)
    shape[axis] = shape[axis] * 2
    return jnp.stack([lower, higher], axis=axis + 1).reshape(shape)


def explode(coarse_pad):
    tall = jnp.concatenate([coarse_pad[..., :1], coarse_pad, coarse_pad[..., -1:]], axis=3)
    return refine_axis(refine_axis(refine_axis(tall, 1), 2), 3)


def coalesce(fine_values):
    count, size_x, size_y, height = fine_values.shape
    shaped = fine_values.reshape(count, size_x // 2, 2, size_y // 2, 2, height // 2, 2)
    return jnp.mean(shaped, axis=(2, 4, 6))


def coarsen(flags):
    size_x, size_y, height = flags.shape
    shaped = flags.reshape(size_x // 2, 2, size_y // 2, 2, height // 2, 2)
    return jnp.max(shaped, axis=(1, 3, 5))


def wrap_span(values, axis):
    length = values.shape[axis]
    return jnp.concatenate([lax.slice_in_dim(values, length - 1, length, axis=axis), values,
                            lax.slice_in_dim(values, 0, 1, axis=axis)], axis=axis)


def reference(fine_pops, coarse_pops, obstacle, block_level, relax_rates):
    fine_rates = relax_rates.reshape(3, 3, 3)
    coarse_rates = 1.0 / (2.0 / fine_rates - 0.5)
    half_x = BX // 2
    level_fine = jnp.repeat(block_level, BY, axis=1)
    level_coarse = jnp.repeat(block_level, BY // 2, axis=1)
    coarse_walls = coarsen(obstacle)

    def slab_rows(slab):
        rows = ((jnp.arange(BX + 2, dtype=jnp.int32) + slab * BX - 1) % NX).astype(jnp.int32)
        coarse_rows = ((jnp.arange(half_x + 4, dtype=jnp.int32) + slab * half_x - 2) % (NX // 2)).astype(jnp.int32)
        coarse_pad = wrap_span(jnp.take(coarse_pops, coarse_rows, axis=1), 2)
        exploded = explode(coarse_pad)[:, 1:BX + 3]
        fine_rows = jnp.take(fine_pops, rows, axis=1)
        refined = jnp.take(level_fine, (rows // BX).astype(jnp.int32), axis=0) == 1
        active = jnp.where(refined[None, :, :, None], fine_rows, exploded)
        padded = wrap_span(active, 2)
        walls = wrap_span(jnp.take(obstacle, rows, axis=0), 1) == 1
        passed = stream_pull(padded, walls)
        fine_new = jnp.where(walls[None, 1:-1, 1:-1], active[:, 1:-1], collide(passed, fine_rates))
        fine_next = jnp.where(refined[None, 1:-1, :, None], fine_new, exploded[:, 1:-1])
        coarse_mid = coarse_pad[:, 1:-1]
        coarse_flags = wrap_span(jnp.take(coarse_walls, coarse_rows[1:-1], axis=0), 1) == 1
        coarse_passed = stream_pull(coarse_mid, coarse_flags)
        coarse_new = jnp.where(coarse_flags[None, 1:-1, 1:-1], coarse_mid[:, 1:-1, 1:-1],
                               collide(coarse_passed, coarse_rates))
        coarse_refined = jnp.take(level_coarse, slab, axis=0) == 1
        coarse_next = jnp.where(coarse_refined[None, None, :, None], coalesce(fine_next), coarse_new)
        return fine_next, coarse_next

    fine_all, coarse_all = lax.map(slab_rows, jnp.arange(N_STREAM, dtype=jnp.int32))
    fine_next = jnp.moveaxis(fine_all, 0, 1).reshape(27, NX, NY, BZ)
    coarse_next = jnp.moveaxis(coarse_all, 0, 1).reshape(27, NX // 2, NY // 2, BZ // 2)
    return fine_next, coarse_next
```

```python
import functools

import jax
import jax.numpy as jnp
from jax import lax
from jax.experimental import pallas as pl
from jax.experimental.pallas import tpu as pltpu
from jax.sharding import PartitionSpec as P

MESH = pl.DeviceIdType.MESH
F32 = jnp.float32
FACES = ((-1, 0), (1, 0), (0, -1), (0, 1))
CORNERS = ((-1, -1), (-1, 1), (1, -1), (1, 1))


def face_pops(side):
    dx, dy = side
    return [q for q in range(27) if (q // 9 - 1 == -dx if dx else q // 3 % 3 - 1 == -dy)]


def corner_start(side):
    dx, dy = side
    return 9 * (1 - dx) + 3 * (1 - dy)


def face_cells(side):
    dx, dy = side
    return [(1 - dx, j) for j in range(3)] if dx else [(i, 1 - dy) for i in range(3)]


def end_pops(side):
    dx, dy = side
    return [face_pops((0, s) if dx else (s, 0)) for s in (-1, 1)]


def pick_rows(cell, pops):
    return jnp.concatenate([cell[q : q + 3] for q in pops[::3]], axis=0)


def exchange_kernel(
    n_stream, n_span, fine, coarse, level, turned, faces, corners, own,
    native, levels, face_out, corner_out, load_sem, send_sem, recv_sem,
):
    row, col = lax.axis_index("stream"), lax.axis_index("span")

    def at(side):
        return (lax.rem(row + side[0] + n_stream, n_stream), lax.rem(col + side[1] + n_span, n_span))

    barrier = pltpu.get_barrier_semaphore()
    for side in CORNERS + FACES:
        pl.semaphore_signal(barrier, inc=1, device_id=at(side), device_id_type=MESH)
    loads = [
        pltpu.make_async_copy(fine, native, load_sem.at[0]),
        pltpu.make_async_copy(coarse, own, load_sem.at[1]),
        pltpu.make_async_copy(level, levels, load_sem.at[2]),
    ]
    for load in loads:
        load.start()
    for load in loads:
        load.wait()
    here = levels[row, col]
    for x in range(6):
        turned[:, x + 1, pl.ds(1, 6), :] = jnp.swapaxes(native[x], 0, 1)
    for slot, side in enumerate(FACES):
        dx, dy = side
        to = at((-dx, -dy))
        both = (here == 1) & (levels[to[0], to[1]] == 1)
        cells = [own[i, j] for i, j in face_cells(side)]
        pair = jnp.concatenate([cells[0], cells[1]], axis=1)
        last = jnp.concatenate([cells[2], cells[2]], axis=1)
        blocks = jnp.concatenate([pair, last], axis=0)
        if dx:
            rows = [turned[q, 6 if dx < 0 else 1, pl.ds(1, 6), :] for q in face_pops(side)]
        else:
            rows = [turned[q, pl.ds(1, 6), 6 if dy < 0 else 1, :] for q in face_pops(side)]
        strips = jnp.concatenate(rows, axis=0)
        face_out[slot, pl.ds(0, 54), :] = jnp.where(both, strips, blocks)
        ends = [pick_rows(cell, pops) for cell, pops in zip((cells[0], cells[2]), end_pops(side))]
        face_out[slot, pl.ds(54, 9), :] = jnp.concatenate(ends, axis=1)
    for slot, side in enumerate(CORNERS):
        dx, dy = side
        cell = own[1 - dx, 1 - dy]
        corner_out[slot, pl.ds(0, 14), :] = jnp.concatenate([cell[0:14], cell[13:27]], axis=1)
        corner_out[slot, pl.ds(14, 3), :] = native[
            5 if dx < 0 else 0, 5 if dy < 0 else 0, pl.ds(corner_start(side), 3), :
        ]
    pl.semaphore_wait(barrier, 8)
    copies = []
    for slot, (dx, dy) in enumerate(FACES):
        copies.append(
            pltpu.make_async_remote_copy(
                face_out.at[slot, pl.ds(0, 63)], faces.at[slot, pl.ds(0, 63)],
                send_sem.at[slot], recv_sem.at[slot], device_id=at((-dx, -dy)), device_id_type=MESH,
            )
        )
    for slot, (dx, dy) in enumerate(CORNERS):
        copies.append(
            pltpu.make_async_remote_copy(
                corner_out.at[slot, pl.ds(0, 17)], corners.at[slot, pl.ds(0, 17)],
                send_sem.at[4 + slot], recv_sem.at[4 + slot], device_id=at((-dx, -dy)), device_id_type=MESH,
            )
        )
    for copy in copies:
        copy.start()
    for copy in copies:
        copy.wait()


def exchange(n_stream, n_span, fine, coarse, level):
    anywhere = pl.BlockSpec(memory_space=pl.ANY)
    vmem = pl.BlockSpec(memory_space=pltpu.VMEM)
    return pl.pallas_call(
        functools.partial(exchange_kernel, n_stream, n_span),
        out_shape=(
            jax.ShapeDtypeStruct((27, 8, 8, 128), F32),
            jax.ShapeDtypeStruct((4, 64, 128), F32),
            jax.ShapeDtypeStruct((4, 24, 128), F32),
            jax.ShapeDtypeStruct((3, 3, 27, 64), F32),
        ),
        in_specs=[anywhere] * 3,
        out_specs=(vmem,) * 4,
        scratch_shapes=[
            pltpu.VMEM((6, 6, 27, 128), F32),
            pltpu.SMEM((16, 32), jnp.int32),
            pltpu.VMEM((4, 64, 128), F32),
            pltpu.VMEM((4, 24, 128), F32),
            pltpu.SemaphoreType.DMA((3,)),
            pltpu.SemaphoreType.DMA((8,)),
            pltpu.SemaphoreType.DMA((8,)),
        ],
        compiler_params=pltpu.CompilerParams(
            collective_id=0, has_side_effects=True, vmem_limit_bytes=24 * 2**20
        ),
    )(fine, coarse, level)


def scalars(rates, coarse):
    keep, pull = [], {}
    for q in range(27):
        rate = rates[q]
        if coarse:
            rate = 1.0 / (2.0 / rate - 0.5)
        keep.append((1.0 - rate) * 0.125)
        orders = (q // 9, q // 3 % 3, q % 3)
        if 1 not in orders:
            pull[q] = rate * (0.125 / 3.0 ** orders.count(2))
    return keep, pull


def forward(low, mid, high, speed, total=None):
    pair, diff = high + low, high - low
    if total is None:
        total = pair + 4.0 * mid
    first = diff - speed * total
    return total, first, pair - speed * (diff + first)


def backward(total, first, second, speed):
    slope = first + speed * total
    curve = second + speed * (first + slope)
    return curve - slope, 0.5 * (total - curve), curve + slope


def collide(g, keep, pull):
    t0 = [g[r] + g[18 + r] + 4.0 * g[9 + r] for r in range(9)]
    dx = [g[18 + r] - g[r] for r in range(9)]
    s0 = [t0[c] + t0[6 + c] + 4.0 * t0[3 + c] for c in range(3)]
    dy = [t0[6 + c] - t0[c] for c in range(3)]
    density = s0[0] + s0[2] + 4.0 * s0[1]
    ex = [dx[c] + dx[6 + c] + 4.0 * dx[3 + c] for c in range(3)]
    inverse = 1.0 / density
    ux = (ex[0] + ex[2] + 4.0 * ex[1]) * inverse
    uy = (dy[0] + dy[2] + 4.0 * dy[1]) * inverse
    uz = (s0[2] - s0[0]) * inverse
    k = [None] * 27
    for r in range(9):
        k[r], k[9 + r], k[18 + r] = forward(g[r], g[9 + r], g[18 + r], ux, t0[r])
    for a in range(3):
        for c in range(3):
            i = 9 * a + c
            k[i], k[i + 3], k[i + 6] = forward(k[i], k[i + 3], k[i + 6], uy, s0[c] if a == 0 else None)
    for i in range(0, 27, 3):
        k[i], k[i + 1], k[i + 2] = forward(k[i], k[i + 1], k[i + 2], uz, density if i == 0 else None)
    for q in range(27):
        k[q] = keep[q] * k[q] + pull[q] * density if q in pull else keep[q] * k[q]
    for i in range(0, 27, 3):
        k[i], k[i + 1], k[i + 2] = backward(k[i], k[i + 1], k[i + 2], uz)
    for a in range(3):
        for c in range(3):
            i = 9 * a + c
            k[i], k[i + 3], k[i + 6] = backward(k[i], k[i + 3], k[i + 6], uy)
    for r in range(9):
        k[r], k[9 + r], k[18 + r] = backward(k[r], k[9 + r], k[18 + r], ux)
    return k


def lane(shape):
    return lax.broadcasted_iota(jnp.int32, shape, len(shape) - 1)


def take(values, index):
    return jnp.take_along_axis(values, index, axis=1)


def stretch(values):
    at = lane(values.shape)
    middle = lax.shift_right_logical(at, 1)
    beside = jnp.clip(middle + 2 * (at & 1) - 1, 0, 63)
    return 0.75 * take(values, middle) + 0.25 * take(values, beside)


def shrink(values):
    at = lane(values.shape)
    even = jnp.minimum(2 * at, 126)
    return (take(values, even) + take(values, even + 1)) * 0.125


def mix(near, far):
    return 0.75 * near + 0.25 * far


def step_kernel(
    n_stream, n_span, given, faces, corners, own, obstacle, levels, rates, fine_out, coarse_out, turned,
    halo, tall, blocked, rolled, coarse_blocked,
):
    row, col = lax.axis_index("stream"), lax.axis_index("span")

    def level_at(side):
        return levels[
            lax.rem(row + side[0] + n_stream, n_stream), lax.rem(col + side[1] + n_span, n_span)
        ]

    refined = levels[row, col] == 1

    for i in range(3):
        for j in range(3):
            halo[i + 1, j + 1, pl.ds(0, 27), pl.ds(0, 64)] = own[i, j]
    for slot, (dx, dy) in enumerate(CORNERS):
        both = corners[slot, pl.ds(0, 14), :]
        cell = halo.at[2 + 2 * dx, 2 + 2 * dy]
        cell[pl.ds(13, 14), :] = pltpu.roll(both, 64, 1)
        cell[pl.ds(0, 14), :] = both
    for slot, side in enumerate(FACES):
        dx, dy = side
        spots = [(2 + 2 * dx, 1 + j) if dx else (1 + j, 2 + 2 * dy) for j in range(3)]
        plain = (levels[row, col] == 0) | (level_at(side) == 0)

        @pl.when(plain)
        def _():
            pair = faces[slot, pl.ds(0, 27), :]
            halo[spots[0][0], spots[0][1], pl.ds(0, 27), :] = pair
            halo[spots[1][0], spots[1][1], pl.ds(0, 27), :] = pltpu.roll(pair, 64, 1)
            halo[spots[2][0], spots[2][1], pl.ds(0, 27), :] = faces[slot, pl.ds(27, 27), :]

        @pl.when(jnp.logical_not(plain))
        def _():
            ends = faces[slot, pl.ds(54, 9), :]
            for spot, pops, rows in zip((spots[0], spots[2]), end_pops(side), (ends, pltpu.roll(ends, 64, 1))):
                for n in (0, 3, 6):
                    halo[spot[0], spot[1], pl.ds(pops[n], 3), :] = rows[n : n + 3]

    for i in range(5):
        for j in range(5):
            tall[i, j, pl.ds(0, 27), :] = stretch(halo[i, j, pl.ds(0, 27), :])

    def tall_at(i, j, start, count):
        return tall[i, j, pl.ds(start, count), :]

    @pl.when(refined)
    def _():
        keep, pull = scalars(rates, False)
        for slot, side in enumerate(FACES):
            dx, dy = side
            pops = face_pops(side)
            edge, inner = 2 + 2 * (dx + dy), 2 + (dx + dy)
            rim = 7 if dx + dy > 0 else 0

            def store(n, q, values):
                if dx:
                    turned[q, rim, pl.ds(1, 6), :] = values
                else:
                    turned[q, pl.ds(1, 6), rim, :] = values

            @pl.when(level_at(side) == 1)
            def _():
                for n, q in enumerate(pops):
                    store(n, q, faces[slot, pl.ds(6 * n, 6), :])

            @pl.when(level_at(side) == 0)
            def _():
                first, count = (pops[0], 9) if dx else (0, 27)
                if dx:
                    line = [mix(tall_at(edge, j, first, count), tall_at(inner, j, first, count)) for j in range(5)]
                else:
                    line = [mix(tall_at(i, edge, first, count), tall_at(i, inner, first, count)) for i in range(5)]
                cells = []
                for n in range(6):
                    cells.append(mix(line[n // 2 + 1], line[n // 2 + 2 * (n % 2)]))
                turn = jnp.swapaxes(jnp.stack(cells), 0, 1)
                for n, q in enumerate(pops):
                    store(n, q, turn[q - first])

        for slot, side in enumerate(CORNERS):
            dx, dy = side
            start = corner_start(side)
            ei, ii, ej, ij = 2 + 2 * dx, 2 + dx, 2 + 2 * dy, 2 + dy
            exploded = mix(
                mix(tall_at(ei, ej, start, 3), tall_at(ii, ej, start, 3)),
                mix(tall_at(ei, ij, start, 3), tall_at(ii, ij, start, 3)),
            )
            value = jnp.where(level_at(side) == 1, corners[slot, pl.ds(14, 3), :], exploded)
            for c in range(3):
                turned[start + c, 7 if dx > 0 else 0, pl.ds(7 if dy > 0 else 0, 1), :] = value[c : c + 1]

        blocked[...] = jnp.zeros_like(blocked)
        blocked[pl.ds(1, 6), pl.ds(1, 6), :] = obstacle[...]
        at = lane((8, 128))
        for x in range(8):
            flags = blocked[x]
            rolled[1, x] = flags
            rolled[2, x] = jnp.where(at == 0, 1, pltpu.roll(flags, 1, 1))
            rolled[0, x] = jnp.where(at == 127, 1, pltpu.roll(flags, 127, 1))

        def line(x, carry):
            g, mid = [], []
            for q in range(27):
                ex, ey, ez = q // 9 - 1, q // 3 % 3 - 1, q % 3 - 1
                source = turned[q, x + 1 - ex, pl.ds(1 - ey, 6), :]
                if ez:
                    source = pltpu.roll(source, ez % 128, 1)
                if q == 13:
                    g.append(source)
                    continue
                stop = rolled[ez + 1, x + 1 - ex, pl.ds(1 - ey, 6), :]
                g.append(jnp.where(stop != 0, turned[26 - q, x + 1, pl.ds(1, 6), :], source))
            new = collide(g, keep, pull)
            wall = blocked[x + 1, pl.ds(1, 6), :] != 0
            new = [jnp.where(wall, turned[q, x + 1, pl.ds(1, 6), :], new[q]) for q in range(27)]
            fine_out[x] = jnp.swapaxes(jnp.stack(new), 0, 1)
            return carry

        lax.fori_loop(0, 6, line, 0)
        for i in range(3):
            for j in range(3):
                total = (fine_out[2 * i, 2 * j] + fine_out[2 * i, 2 * j + 1]) + (
                    fine_out[2 * i + 1, 2 * j] + fine_out[2 * i + 1, 2 * j + 1]
                )
                coarse_out[i, j] = shrink(total)[:, :64]

    @pl.when(jnp.logical_not(refined))
    def _():
        for x in range(6):
            line = [
                mix(tall_at(x // 2 + 1, j, 0, 27), tall_at(x // 2 + 2 * (x % 2), j, 0, 27)) for j in range(5)
            ]
            for y in range(6):
                fine_out[x, y] = mix(line[y // 2 + 1], line[y // 2 + 2 * (y % 2)])

        keep, pull = scalars(rates, True)
        flat = turned.reshape(27 * 64, 128)
        for i in range(5):
            cells = jnp.swapaxes(halo[i, :, pl.ds(0, 27), :], 0, 1)
            for q in range(27):
                flat[pl.ds(64 * q + 5 * i, 5), :] = cells[q]
        column = jnp.maximum(
            jnp.maximum(obstacle[2, pl.ds(2, 1), :], obstacle[2, pl.ds(3, 1), :]),
            jnp.maximum(obstacle[3, pl.ds(2, 1), :], obstacle[3, pl.ds(3, 1), :]),
        )
        at = lane((1, 128))
        even = jnp.minimum(2 * at, 126)
        wide = jnp.broadcast_to(column, (8, 128))
        even = jnp.broadcast_to(even, (8, 128))
        flags = jnp.maximum(take(wide, even), take(wide, even + 1))[:1]
        flags = jnp.where(at < 64, flags, 0)
        coarse_blocked[...] = jnp.zeros_like(coarse_blocked)
        coarse_blocked[1, pl.ds(12, 1), :] = flags
        high = lane((32, 128))
        coarse_blocked[2] = jnp.where(high == 0, 1, pltpu.roll(coarse_blocked[1], 1, 1))
        coarse_blocked[0] = jnp.where(high == 63, 1, pltpu.roll(coarse_blocked[1], 127, 1))
        g = []
        for q in range(27):
            ex, ey, ez = q // 9 - 1, q // 3 % 3 - 1, q % 3 - 1
            start = 6 - 5 * ex - ey
            source = flat[pl.ds(64 * q + start, 13), :]
            if ez:
                source = pltpu.roll(source, ez % 128, 1)
            if q != 13:
                stop = coarse_blocked[ez + 1, pl.ds(start, 13), :]
                source = jnp.where(stop != 0, flat[pl.ds(64 * (26 - q) + 6, 13), :], source)
            g.append(source)
        new = collide(g, keep, pull)
        wall = coarse_blocked[1, pl.ds(6, 13), :] != 0
        new = [jnp.where(wall, flat[pl.ds(64 * q + 6, 13), :], new[q]) for q in range(27)]
        turn = jnp.swapaxes(jnp.stack(new), 0, 1)
        for i in range(3):
            for j in range(3):
                coarse_out[i, j] = turn[5 * i + j][:, :64]


def step(n_stream, n_span, turned, faces, corners, own, obstacle, level, rates):
    vmem = pl.BlockSpec(memory_space=pltpu.VMEM)
    smem = pl.BlockSpec(memory_space=pltpu.SMEM)
    return pl.pallas_call(
        functools.partial(step_kernel, n_stream, n_span),
        out_shape=(
            jax.ShapeDtypeStruct((6, 6, 27, 128), F32),
            jax.ShapeDtypeStruct((3, 3, 27, 64), F32),
            jax.ShapeDtypeStruct((27, 8, 8, 128), F32),
        ),
        in_specs=[vmem] * 5 + [smem] * 2,
        out_specs=(vmem,) * 3,
        input_output_aliases={0: 2},
        scratch_shapes=[
            pltpu.VMEM((5, 5, 32, 128), F32),
            pltpu.VMEM((5, 5, 32, 128), F32),
            pltpu.VMEM((8, 8, 128), jnp.int32),
            pltpu.VMEM((3, 8, 8, 128), jnp.int32),
            pltpu.VMEM((3, 32, 128), jnp.int32),
        ],
        compiler_params=pltpu.CompilerParams(vmem_limit_bytes=24 * 2**20),
    )(turned, faces, corners, own, obstacle, level, rates)


def solution(mesh):
    n_stream, n_span = mesh.shape["stream"], mesh.shape["span"]

    def local(fine_pops, coarse_pops, obstacle, block_level, relax_rates):
        fine = jnp.transpose(fine_pops, (1, 2, 0, 3))
        coarse = jnp.transpose(coarse_pops, (1, 2, 0, 3))
        turned, faces, corners, own = exchange(n_stream, n_span, fine, coarse, block_level)
        fine_next, coarse_next, _ = step(
            n_stream, n_span, turned, faces, corners, own, obstacle, block_level, relax_rates
        )
        return jnp.transpose(fine_next, (2, 0, 1, 3)), jnp.transpose(coarse_next, (2, 0, 1, 3))

    placed = P(None, "stream", "span", None)
    return jax.shard_map(
        local,
        mesh=mesh,
        in_specs=(placed, placed, P("stream", "span", None), P(), P()),
        out_specs=(placed, placed),
        check_vma=False,
    )
```

```python
import functools

import jax
import jax.numpy as jnp
from jax import lax
from jax.experimental import pallas as pl
from jax.experimental.pallas import tpu as pltpu
from jax.sharding import PartitionSpec as P

MESH = pl.DeviceIdType.MESH
F32 = jnp.float32
FACES = ((-1, 0), (1, 0), (0, -1), (0, 1))
CORNERS = ((-1, -1), (-1, 1), (1, -1), (1, 1))


def face_pops(side):
    dx, dy = side
    return [q for q in range(27) if (q // 9 - 1 == -dx if dx else q // 3 % 3 - 1 == -dy)]


def corner_start(side):
    dx, dy = side
    return 9 * (1 - dx) + 3 * (1 - dy)


def face_cells(side):
    dx, dy = side
    return [(1 - dx, j) for j in range(3)] if dx else [(i, 1 - dy) for i in range(3)]


def end_pops(side):
    dx, dy = side
    return [face_pops((0, s) if dx else (s, 0)) for s in (-1, 1)]


def pick_rows(cell, pops):
    return jnp.concatenate([cell[q : q + 3] for q in pops[::3]], axis=0)


def exchange_kernel(
    n_stream, n_span, fine, coarse, obstacle, level, rates,
    turned, faces, corners, tall, own, flags, table, around,
    native, levels, speeds, face_out, corner_out, load_sem, send_sem, recv_sem,
):
    row, col = lax.axis_index("stream"), lax.axis_index("span")

    def at(side):
        return (lax.rem(row + side[0] + n_stream, n_stream), lax.rem(col + side[1] + n_span, n_span))

    barrier = pltpu.get_barrier_semaphore()
    loads = [
        pltpu.make_async_copy(fine, native, load_sem.at[0]),
        pltpu.make_async_copy(coarse, own, load_sem.at[1]),
        pltpu.make_async_copy(level, levels, load_sem.at[2]),
        pltpu.make_async_copy(obstacle, flags, load_sem.at[3]),
        pltpu.make_async_copy(rates, speeds, load_sem.at[4]),
    ]
    for load in loads:
        load.start()
    for side in CORNERS + FACES:
        pl.semaphore_signal(barrier, inc=1, device_id=at(side), device_id_type=MESH)
    for load in loads[:3]:
        load.wait()
    here = levels[row, col]
    there = [levels[at(side)[0], at(side)[1]] for side in FACES + CORNERS]
    for slot, side in enumerate(CORNERS):
        dx, dy = side
        cell = own[1 - dx, 1 - dy]
        corner_out[slot, pl.ds(0, 14), :] = jnp.concatenate([cell[0:14], cell[13:27]], axis=1)
        corner_out[slot, pl.ds(14, 3), :] = native[
            5 if dx < 0 else 0, 5 if dy < 0 else 0, pl.ds(corner_start(side), 3), :
        ]
    for slot, side in enumerate(FACES):
        dx, dy = side
        both = (here == 1) & (there[FACES.index((-dx, -dy))] == 1)
        cells = [own[i, j] for i, j in face_cells(side)]
        face_out[slot, pl.ds(0, 27), :] = jnp.concatenate([cells[0], cells[1]], axis=1)
        face_out[slot, pl.ds(27, 27), :] = jnp.concatenate([cells[2], cells[2]], axis=1)
        edge = native[5 if dx < 0 else 0] if dx else native[:, 5 if dy < 0 else 0]
        edge = jnp.swapaxes(edge, 0, 1)
        for n, q in enumerate(face_pops(side)):
            spot = face_out.at[slot, pl.ds(6 * n, 6)]
            spot[...] = jnp.where(both, edge[q], spot[...])
        ends = [pick_rows(cell, pops) for cell, pops in zip((cells[0], cells[2]), end_pops(side))]
        face_out[slot, pl.ds(54, 9), :] = jnp.concatenate(ends, axis=1)
    pl.semaphore_wait(barrier, 8)
    copies = []
    for slot, (dx, dy) in enumerate(CORNERS):
        copies.append(
            pltpu.make_async_remote_copy(
                corner_out.at[slot, pl.ds(0, 17)], corners.at[slot, pl.ds(0, 17)],
                send_sem.at[4 + slot], recv_sem.at[4 + slot], device_id=at((-dx, -dy)), device_id_type=MESH,
            )
        )
    for slot, (dx, dy) in enumerate(FACES):
        copies.append(
            pltpu.make_async_remote_copy(
                face_out.at[slot, pl.ds(0, 63)], faces.at[slot, pl.ds(0, 63)],
                send_sem.at[slot], recv_sem.at[slot], device_id=at((-dx, -dy)), device_id_type=MESH,
            )
        )
    for copy in copies:
        copy.start()
    for x in range(6):
        turned[:, x + 1, pl.ds(1, 6), :] = jnp.swapaxes(native[x], 0, 1)
    for i in range(3):
        for j in range(3):
            cell = own[i, j]
            tall[i, j] = stretch(jnp.concatenate([cell, cell], axis=1))
    for n, value in enumerate([here] + there):
        around[n] = jnp.full((8, 128), value, jnp.int32)
    for load in loads[3:]:
        load.wait()
    for q in range(27):
        orders = (q // 9, q // 3 % 3, q % 3)
        share = 0.0 if 1 in orders else 0.125 / 3.0 ** orders.count(2)
        fine_rate = jnp.full((1, 128), speeds[q], F32)
        for n, rate in enumerate((fine_rate, 1.0 / (2.0 / fine_rate - 0.5))):
            table[n, 0, pl.ds(q, 1), :] = (1.0 - rate) * 0.125
            table[n, 1, pl.ds(q, 1), :] = rate * share
    for copy in copies:
        copy.wait()


def exchange(n_stream, n_span, *args):
    hbm = pl.BlockSpec(memory_space=pltpu.HBM)
    vmem = pl.BlockSpec(memory_space=pltpu.VMEM)
    return pl.pallas_call(
        functools.partial(exchange_kernel, n_stream, n_span),
        out_shape=(
            jax.ShapeDtypeStruct((27, 8, 8, 128), F32),
            jax.ShapeDtypeStruct((4, 64, 128), F32),
            jax.ShapeDtypeStruct((4, 24, 128), F32),
            jax.ShapeDtypeStruct((3, 3, 27, 128), F32),
            jax.ShapeDtypeStruct((3, 3, 27, 64), F32),
            jax.ShapeDtypeStruct((6, 6, 128), jnp.int32),
            jax.ShapeDtypeStruct((2, 2, 32, 128), F32),
            jax.ShapeDtypeStruct((9, 8, 128), jnp.int32),
        ),
        in_specs=[hbm] * 5,
        out_specs=(vmem,) * 8,
        scratch_shapes=[
            pltpu.VMEM((6, 6, 27, 128), F32),
            pltpu.SMEM((16, 32), jnp.int32),
            pltpu.SMEM((27,), F32),
            pltpu.VMEM((4, 64, 128), F32),
            pltpu.VMEM((4, 24, 128), F32),
            pltpu.SemaphoreType.DMA((5,)),
            pltpu.SemaphoreType.DMA((8,)),
            pltpu.SemaphoreType.DMA((8,)),
        ],
        compiler_params=pltpu.CompilerParams(
            collective_id=0, has_side_effects=True, vmem_limit_bytes=24 * 2**20
        ),
    )(*args)


def forward(low, mid, high, speed, total=None):
    pair, diff = high + low, high - low
    if total is None:
        total = pair + 4.0 * mid
    first = diff - speed * total
    return total, first, pair - speed * (diff + first)


def backward(total, first, second, speed):
    slope = first + speed * total
    curve = second + speed * (first + slope)
    return curve - slope, 0.5 * (total - curve), curve + slope


def collide(g, keep, pull):
    t0 = [g[r] + g[18 + r] + 4.0 * g[9 + r] for r in range(9)]
    dx = [g[18 + r] - g[r] for r in range(9)]
    s0 = [t0[c] + t0[6 + c] + 4.0 * t0[3 + c] for c in range(3)]
    dy = [t0[6 + c] - t0[c] for c in range(3)]
    density = s0[0] + s0[2] + 4.0 * s0[1]
    ex = [dx[c] + dx[6 + c] + 4.0 * dx[3 + c] for c in range(3)]
    inverse = 1.0 / density
    ux = (ex[0] + ex[2] + 4.0 * ex[1]) * inverse
    uy = (dy[0] + dy[2] + 4.0 * dy[1]) * inverse
    uz = (s0[2] - s0[0]) * inverse
    k = [None] * 27
    for r in range(9):
        k[r], k[9 + r], k[18 + r] = forward(g[r], g[9 + r], g[18 + r], ux, t0[r])
    for a in range(3):
        for c in range(3):
            i = 9 * a + c
            k[i], k[i + 3], k[i + 6] = forward(k[i], k[i + 3], k[i + 6], uy, s0[c] if a == 0 else None)
    for i in range(0, 27, 3):
        k[i], k[i + 1], k[i + 2] = forward(k[i], k[i + 1], k[i + 2], uz, density if i == 0 else None)
    for q in range(27):
        k[q] = keep[q] * k[q] if 1 in (q // 9, q // 3 % 3, q % 3) else keep[q] * k[q] + pull[q] * density
    for i in range(0, 27, 3):
        k[i], k[i + 1], k[i + 2] = backward(k[i], k[i + 1], k[i + 2], uz)
    for a in range(3):
        for c in range(3):
            i = 9 * a + c
            k[i], k[i + 3], k[i + 6] = backward(k[i], k[i + 3], k[i + 6], uy)
    for r in range(9):
        k[r], k[9 + r], k[18 + r] = backward(k[r], k[9 + r], k[18 + r], ux)
    return k


def lane(shape):
    return lax.broadcasted_iota(jnp.int32, shape, len(shape) - 1)


def take(values, index):
    return jnp.take_along_axis(values, index, axis=1)


def stretch(values):
    at = lane(values.shape)
    middle = lax.shift_right_logical(at, 1)
    beside = jnp.clip(middle + 2 * (at & 1) - 1, 0, 63)
    return 0.75 * take(values, middle) + 0.25 * take(values, beside)


def shrink(values):
    at = lane(values.shape)
    even = jnp.minimum(2 * at, 126)
    return (take(values, even) + take(values, even + 1)) * 0.125


def mix(near, far):
    return 0.75 * near + 0.25 * far


def step_kernel(
    given, faces, corners, own_tall, own, obstacle, table, around, fine_next, coarse_next, turned,
    halo, tall, blocked, rolled, coarse_blocked, fine_out, coarse_out, fine_sem, coarse_sem,
):
    def level(n, rows):
        return around[n, pl.ds(0, rows), :] == 1

    def fine_copy(i):
        return pltpu.make_async_copy(fine_out.at[pl.ds(2 * i, 2)], fine_next.at[pl.ds(2 * i, 2)], fine_sem.at[i])

    def coarse_copy():
        return pltpu.make_async_copy(coarse_out, coarse_next, coarse_sem)

    def rates(n):
        return [table[n, 0, pl.ds(q, 1), :] for q in range(27)], [table[n, 1, pl.ds(q, 1), :] for q in range(27)]

    refined = jnp.max(around[0]) == 1

    def halo_cells(side):
        dx, dy = side
        return [(2 + 2 * dx, 1 + j) if dx else (1 + j, 2 + 2 * dy) for j in range(3)]

    def received(raw):
        for slot, (dx, dy) in enumerate(CORNERS):
            both = corners[slot, pl.ds(0, 14), :]
            other = pltpu.roll(both, 64, 1)
            if raw:
                halo[2 + 2 * dx, 2 + 2 * dy, pl.ds(13, 14), :] = other
                halo[2 + 2 * dx, 2 + 2 * dy, pl.ds(0, 14), :] = both
            tall[2 + 2 * dx, 2 + 2 * dy, pl.ds(13, 14), :] = stretch(other)
            tall[2 + 2 * dx, 2 + 2 * dy, pl.ds(0, 14), :] = stretch(both)
        for slot, side in enumerate(FACES):
            spots = halo_cells(side)
            pair = faces[slot, pl.ds(0, 27), :]
            for spot, cell in zip(spots, (pair, pltpu.roll(pair, 64, 1), faces[slot, pl.ds(27, 27), :])):
                if raw:
                    halo[spot[0], spot[1], pl.ds(0, 27), :] = cell
                tall[spot[0], spot[1], pl.ds(0, 27), :] = stretch(cell)
        for i in range(3):
            for j in range(3):
                if raw:
                    halo[i + 1, j + 1, pl.ds(0, 27), pl.ds(0, 64)] = own[i, j]

    def tall_at(i, j, start, count):
        if 0 < i < 4 and 0 < j < 4:
            return own_tall[i - 1, j - 1, pl.ds(start, count), :]
        return tall[i, j, pl.ds(start, count), :]

    @pl.when(refined)
    def _():
        received(False)
        for slot, side in enumerate(FACES):
            ends = faces[slot, pl.ds(54, 9), :]
            spots = halo_cells(side)
            take_ends = level(1 + slot, 1)
            for spot, pops, rows in zip((spots[0], spots[2]), end_pops(side), (ends, pltpu.roll(ends, 64, 1))):
                rows = stretch(rows)
                for n in (0, 3, 6):
                    place = tall.at[spot[0], spot[1], pl.ds(pops[n], 3)]
                    place[...] = jnp.where(take_ends, rows[n : n + 3], place[...])
        for slot, side in enumerate(FACES):
            dx, dy = side
            pops = face_pops(side)
            edge, inner = 2 + 2 * (dx + dy), 2 + (dx + dy)
            rim = 7 if dx + dy > 0 else 0
            first, count = (pops[0], 9) if dx else (0, 27)
            if dx:
                line = [mix(tall_at(edge, j, first, count), tall_at(inner, j, first, count)) for j in range(5)]
            else:
                line = [mix(tall_at(i, edge, first, count), tall_at(i, inner, first, count)) for i in range(5)]
            cells = []
            for n in range(6):
                cells.append(mix(line[n // 2 + 1], line[n // 2 + 2 * (n % 2)]))
            turn = jnp.swapaxes(jnp.stack(cells), 0, 1)
            fine_there = level(1 + slot, 6)
            for n, q in enumerate(pops):
                values = jnp.where(fine_there, faces[slot, pl.ds(6 * n, 6), :], turn[q - first])
                if dx:
                    turned[q, rim, pl.ds(1, 6), :] = values
                else:
                    turned[q, pl.ds(1, 6), rim, :] = values

        for slot, side in enumerate(CORNERS):
            dx, dy = side
            start = corner_start(side)
            ei, ii, ej, ij = 2 + 2 * dx, 2 + dx, 2 + 2 * dy, 2 + dy
            exploded = mix(
                mix(tall_at(ei, ej, start, 3), tall_at(ii, ej, start, 3)),
                mix(tall_at(ei, ij, start, 3), tall_at(ii, ij, start, 3)),
            )
            value = jnp.where(level(5 + slot, 3), corners[slot, pl.ds(14, 3), :], exploded)
            for c in range(3):
                turned[start + c, 7 if dx > 0 else 0, pl.ds(7 if dy > 0 else 0, 1), :] = value[c : c + 1]

        blocked[...] = jnp.zeros_like(blocked)
        blocked[pl.ds(1, 6), pl.ds(1, 6), :] = obstacle[...]
        at = lane((8, 128))
        for x in range(8):
            flags = blocked[x]
            rolled[1, x] = flags
            rolled[2, x] = jnp.where(at == 0, 1, pltpu.roll(flags, 1, 1))
            rolled[0, x] = jnp.where(at == 127, 1, pltpu.roll(flags, 127, 1))

        def line(x):
            keep, pull = rates(0)
            g = []
            for q in range(27):
                ex, ey, ez = q // 9 - 1, q // 3 % 3 - 1, q % 3 - 1
                source = turned[q, x + 1 - ex, pl.ds(1 - ey, 6), :]
                if ez:
                    source = pltpu.roll(source, ez % 128, 1)
                if q == 13:
                    g.append(source)
                    continue
                stop = rolled[ez + 1, x + 1 - ex, pl.ds(1 - ey, 6), :]
                g.append(jnp.where(stop != 0, turned[26 - q, x + 1, pl.ds(1, 6), :], source))
            new = collide(g, keep, pull)
            wall = blocked[x + 1, pl.ds(1, 6), :] != 0
            new = [jnp.where(wall, turned[q, x + 1, pl.ds(1, 6), :], new[q]) for q in range(27)]
            fine_out[x] = jnp.swapaxes(jnp.stack(new), 0, 1)

        def lines(i, carry):
            line(2 * i)
            line(2 * i + 1)
            fine_copy(i).start()
            for j in range(3):
                total = (fine_out[2 * i, 2 * j] + fine_out[2 * i, 2 * j + 1]) + (
                    fine_out[2 * i + 1, 2 * j] + fine_out[2 * i + 1, 2 * j + 1]
                )
                coarse_out[i, j] = shrink(total)[:, :64]
            return carry

        lax.fori_loop(0, 3, lines, 0)
        coarse_copy().start()

    @pl.when(jnp.logical_not(refined))
    def _():
        received(True)
        for i in range(3):
            for x in (2 * i, 2 * i + 1):
                line = [mix(tall_at(i + 1, j, 0, 27), tall_at(i + 2 * (x % 2), j, 0, 27)) for j in range(5)]
                for y in range(6):
                    fine_out[x, y] = mix(line[y // 2 + 1], line[y // 2 + 2 * (y % 2)])
            fine_copy(i).start()

        keep, pull = rates(1)
        flat = turned.reshape(27 * 64, 128)
        for i in range(5):
            cells = jnp.swapaxes(halo[i, :, pl.ds(0, 27), :], 0, 1)
            for q in range(27):
                flat[pl.ds(64 * q + 5 * i, 5), :] = cells[q]
        column = jnp.maximum(
            jnp.maximum(obstacle[2, pl.ds(2, 1), :], obstacle[2, pl.ds(3, 1), :]),
            jnp.maximum(obstacle[3, pl.ds(2, 1), :], obstacle[3, pl.ds(3, 1), :]),
        )
        wide = jnp.broadcast_to(column, (8, 128))
        at = lane((8, 128))
        even = jnp.minimum(2 * at, 126)
        flags = jnp.maximum(take(wide, even), take(wide, even + 1))
        flags = jnp.where(at < 64, flags, 0)
        coarse_blocked[...] = jnp.zeros_like(coarse_blocked)
        coarse_blocked[1, pl.ds(12, 1), :] = flags[:1]
        high = lane((32, 128))
        coarse_blocked[2] = jnp.where(high == 0, 1, pltpu.roll(coarse_blocked[1], 1, 1))
        coarse_blocked[0] = jnp.where(high == 63, 1, pltpu.roll(coarse_blocked[1], 127, 1))
        g = []
        for q in range(27):
            ex, ey, ez = q // 9 - 1, q // 3 % 3 - 1, q % 3 - 1
            start = 6 - 5 * ex - ey
            source = flat[pl.ds(64 * q + start, 13), :]
            if ez:
                source = pltpu.roll(source, ez % 128, 1)
            if q != 13:
                stop = coarse_blocked[ez + 1, pl.ds(start, 13), :]
                source = jnp.where(stop != 0, flat[pl.ds(64 * (26 - q) + 6, 13), :], source)
            g.append(source)
        new = collide(g, keep, pull)
        wall = coarse_blocked[1, pl.ds(6, 13), :] != 0
        new = [jnp.where(wall, flat[pl.ds(64 * q + 6, 13), :], new[q]) for q in range(27)]
        turn = jnp.swapaxes(jnp.stack(new), 0, 1)
        for i in range(3):
            for j in range(3):
                coarse_out[i, j] = turn[5 * i + j][:, :64]
        coarse_copy().start()

    for i in range(3):
        fine_copy(i).wait()
    coarse_copy().wait()


def step(*args):
    vmem = pl.BlockSpec(memory_space=pltpu.VMEM)
    hbm = pl.BlockSpec(memory_space=pltpu.HBM)
    return pl.pallas_call(
        step_kernel,
        out_shape=(
            jax.ShapeDtypeStruct((6, 6, 27, 128), F32),
            jax.ShapeDtypeStruct((3, 3, 27, 64), F32),
            jax.ShapeDtypeStruct((27, 8, 8, 128), F32),
        ),
        in_specs=[vmem] * 8,
        out_specs=(hbm, hbm, vmem),
        input_output_aliases={0: 2},
        scratch_shapes=[
            pltpu.VMEM((5, 5, 32, 128), F32),
            pltpu.VMEM((5, 5, 32, 128), F32),
            pltpu.VMEM((8, 8, 128), jnp.int32),
            pltpu.VMEM((3, 8, 8, 128), jnp.int32),
            pltpu.VMEM((3, 32, 128), jnp.int32),
            pltpu.VMEM((6, 6, 27, 128), F32),
            pltpu.VMEM((3, 3, 27, 64), F32),
            pltpu.SemaphoreType.DMA((3,)),
            pltpu.SemaphoreType.DMA,
        ],
        compiler_params=pltpu.CompilerParams(vmem_limit_bytes=24 * 2**20),
    )(*args)


def solution(mesh):
    n_stream, n_span = mesh.shape["stream"], mesh.shape["span"]

    def local(fine_pops, coarse_pops, obstacle, block_level, relax_rates):
        fine = jnp.transpose(fine_pops, (1, 2, 0, 3))
        coarse = jnp.transpose(coarse_pops, (1, 2, 0, 3))
        ready = exchange(n_stream, n_span, fine, coarse, obstacle, block_level, relax_rates)
        fine_next, coarse_next, _ = step(*ready)
        return jnp.transpose(fine_next, (2, 0, 1, 3)), jnp.transpose(coarse_next, (2, 0, 1, 3))

    placed = P(None, "stream", "span", None)
    return jax.shard_map(
        local,
        mesh=mesh,
        in_specs=(placed, placed, P("stream", "span", None), P(), P()),
        out_specs=(placed, placed),
        check_vma=False,
    )
```

```python
import functools

import jax
import jax.numpy as jnp
from jax import lax
from jax.experimental import pallas as pl
from jax.experimental.pallas import tpu as pltpu
from jax.sharding import PartitionSpec as P

MESH = pl.DeviceIdType.MESH
F32 = jnp.float32
FACES = ((-1, 0), (1, 0), (0, -1), (0, 1))
CORNERS = ((-1, -1), (-1, 1), (1, -1), (1, 1))


def face_pops(side):
    dx, dy = side
    return [q for q in range(27) if (q // 9 - 1 == -dx if dx else q // 3 % 3 - 1 == -dy)]


def corner_start(side):
    dx, dy = side
    return 9 * (1 - dx) + 3 * (1 - dy)


def face_cells(side):
    dx, dy = side
    return [(1 - dx, j) for j in range(3)] if dx else [(i, 1 - dy) for i in range(3)]


def end_pops(side):
    dx, dy = side
    return [face_pops((0, s) if dx else (s, 0)) for s in (-1, 1)]


def pick_rows(cell, pops):
    return jnp.concatenate([cell[q : q + 3] for q in pops[::3]], axis=0)


def exchange_kernel(
    n_stream, n_span, fine, coarse, obstacle, level, rates,
    turned, faces, corners, tall, own, flags, table, around,
    native, levels, speeds, face_out, corner_out, load_sem, send_sem, recv_sem,
):
    row, col = lax.axis_index("stream"), lax.axis_index("span")

    def at(side):
        return (lax.rem(row + side[0] + n_stream, n_stream), lax.rem(col + side[1] + n_span, n_span))

    barrier = pltpu.get_barrier_semaphore()
    loads = [
        pltpu.make_async_copy(fine, native, load_sem.at[0]),
        pltpu.make_async_copy(coarse, own, load_sem.at[1]),
        pltpu.make_async_copy(level, levels, load_sem.at[2]),
        pltpu.make_async_copy(obstacle, flags, load_sem.at[3]),
        pltpu.make_async_copy(rates, speeds, load_sem.at[4]),
    ]
    for load in loads:
        load.start()
    for side in CORNERS + FACES:
        pl.semaphore_signal(barrier, inc=1, device_id=at(side), device_id_type=MESH)
    for load in loads[:3]:
        load.wait()
    here = levels[row, col]
    there = [levels[at(side)[0], at(side)[1]] for side in FACES + CORNERS]
    for slot, side in enumerate(CORNERS):
        dx, dy = side
        cell = own[1 - dx, 1 - dy]
        corner_out[slot, pl.ds(0, 14), :] = jnp.concatenate([cell[0:14], cell[13:27]], axis=1)
        corner_out[slot, pl.ds(14, 3), :] = native[
            5 if dx < 0 else 0, 5 if dy < 0 else 0, pl.ds(corner_start(side), 3), :
        ]
    for slot, side in enumerate(FACES):
        dx, dy = side
        both = (here == 1) & (there[FACES.index((-dx, -dy))] == 1)
        cells = [own[i, j] for i, j in face_cells(side)]
        face_out[slot, pl.ds(0, 27), :] = jnp.concatenate([cells[0], cells[1]], axis=1)
        face_out[slot, pl.ds(27, 27), :] = jnp.concatenate([cells[2], cells[2]], axis=1)
        edge = native[5 if dx < 0 else 0] if dx else native[:, 5 if dy < 0 else 0]
        edge = jnp.swapaxes(edge, 0, 1)
        for n, q in enumerate(face_pops(side)):
            spot = face_out.at[slot, pl.ds(6 * n, 6)]
            spot[...] = jnp.where(both, edge[q], spot[...])
        ends = [pick_rows(cell, pops) for cell, pops in zip((cells[0], cells[2]), end_pops(side))]
        face_out[slot, pl.ds(54, 9), :] = jnp.concatenate(ends, axis=1)
    pl.semaphore_wait(barrier, 8)
    copies = []
    for slot, (dx, dy) in enumerate(CORNERS):
        copies.append(
            pltpu.make_async_remote_copy(
                corner_out.at[slot, pl.ds(0, 17)], corners.at[slot, pl.ds(0, 17)],
                send_sem.at[4 + slot], recv_sem.at[4 + slot], device_id=at((-dx, -dy)), device_id_type=MESH,
            )
        )
    for slot, (dx, dy) in enumerate(FACES):
        copies.append(
            pltpu.make_async_remote_copy(
                face_out.at[slot, pl.ds(0, 63)], faces.at[slot, pl.ds(0, 63)],
                send_sem.at[slot], recv_sem.at[slot], device_id=at((-dx, -dy)), device_id_type=MESH,
            )
        )
    for copy in copies:
        copy.start()
    for x in range(6):
        turned[:, x + 1, pl.ds(1, 6), :] = jnp.swapaxes(native[x], 0, 1)
    for i in range(3):
        for j in range(3):
            cell = own[i, j]
            tall[i, j] = stretch(jnp.concatenate([cell, cell], axis=1))
    for n, value in enumerate([here] + there):
        around[n] = jnp.full((8, 128), value, jnp.int32)
    for load in loads[3:]:
        load.wait()
    for q in range(27):
        orders = (q // 9, q // 3 % 3, q % 3)
        share = 0.0 if 1 in orders else 0.125 / 3.0 ** orders.count(2)
        fine_rate = jnp.full((1, 128), speeds[q], F32)
        for n, rate in enumerate((fine_rate, 1.0 / (2.0 / fine_rate - 0.5))):
            table[n, 0, pl.ds(q, 1), :] = (1.0 - rate) * 0.125
            table[n, 1, pl.ds(q, 1), :] = rate * share
    for copy in copies:
        copy.wait()


def exchange(n_stream, n_span, *args):
    hbm = pl.BlockSpec(memory_space=pltpu.HBM)
    vmem = pl.BlockSpec(memory_space=pltpu.VMEM)
    return pl.pallas_call(
        functools.partial(exchange_kernel, n_stream, n_span),
        out_shape=(
            jax.ShapeDtypeStruct((27, 8, 8, 128), F32),
            jax.ShapeDtypeStruct((4, 64, 128), F32),
            jax.ShapeDtypeStruct((4, 24, 128), F32),
            jax.ShapeDtypeStruct((3, 3, 27, 128), F32),
            jax.ShapeDtypeStruct((3, 3, 27, 64), F32),
            jax.ShapeDtypeStruct((6, 6, 128), jnp.int32),
            jax.ShapeDtypeStruct((2, 2, 32, 128), F32),
            jax.ShapeDtypeStruct((9, 8, 128), jnp.int32),
        ),
        in_specs=[hbm] * 5,
        out_specs=(vmem,) * 8,
        scratch_shapes=[
            pltpu.VMEM((6, 6, 27, 128), F32),
            pltpu.SMEM((16, 32), jnp.int32),
            pltpu.SMEM((27,), F32),
            pltpu.VMEM((4, 64, 128), F32),
            pltpu.VMEM((4, 24, 128), F32),
            pltpu.SemaphoreType.DMA((5,)),
            pltpu.SemaphoreType.DMA((8,)),
            pltpu.SemaphoreType.DMA((8,)),
        ],
        compiler_params=pltpu.CompilerParams(
            collective_id=0, has_side_effects=True, vmem_limit_bytes=24 * 2**20
        ),
    )(*[pltpu.with_memory_space_constraint(arg, pltpu.HBM) for arg in args])


def forward(low, mid, high, speed, total=None):
    pair, diff = high + low, high - low
    if total is None:
        total = pair + 4.0 * mid
    first = diff - speed * total
    return total, first, pair - speed * (diff + first)


def backward(total, first, second, speed):
    slope = first + speed * total
    curve = second + speed * (first + slope)
    return curve - slope, 0.5 * (total - curve), curve + slope


def collide(g, keep, pull):
    t0 = [g[r] + g[18 + r] + 4.0 * g[9 + r] for r in range(9)]
    dx = [g[18 + r] - g[r] for r in range(9)]
    s0 = [t0[c] + t0[6 + c] + 4.0 * t0[3 + c] for c in range(3)]
    dy = [t0[6 + c] - t0[c] for c in range(3)]
    density = s0[0] + s0[2] + 4.0 * s0[1]
    ex = [dx[c] + dx[6 + c] + 4.0 * dx[3 + c] for c in range(3)]
    inverse = 1.0 / density
    ux = (ex[0] + ex[2] + 4.0 * ex[1]) * inverse
    uy = (dy[0] + dy[2] + 4.0 * dy[1]) * inverse
    uz = (s0[2] - s0[0]) * inverse
    k = [None] * 27
    for r in range(9):
        k[r], k[9 + r], k[18 + r] = forward(g[r], g[9 + r], g[18 + r], ux, t0[r])
    for a in range(3):
        for c in range(3):
            i = 9 * a + c
            k[i], k[i + 3], k[i + 6] = forward(k[i], k[i + 3], k[i + 6], uy, s0[c] if a == 0 else None)
    for i in range(0, 27, 3):
        k[i], k[i + 1], k[i + 2] = forward(k[i], k[i + 1], k[i + 2], uz, density if i == 0 else None)
    for q in range(27):
        k[q] = keep[q] * k[q] if 1 in (q // 9, q // 3 % 3, q % 3) else keep[q] * k[q] + pull[q] * density
    for i in range(0, 27, 3):
        k[i], k[i + 1], k[i + 2] = backward(k[i], k[i + 1], k[i + 2], uz)
    for a in range(3):
        for c in range(3):
            i = 9 * a + c
            k[i], k[i + 3], k[i + 6] = backward(k[i], k[i + 3], k[i + 6], uy)
    for r in range(9):
        k[r], k[9 + r], k[18 + r] = backward(k[r], k[9 + r], k[18 + r], ux)
    return k


def lane(shape):
    return lax.broadcasted_iota(jnp.int32, shape, len(shape) - 1)


def take(values, index):
    return jnp.take_along_axis(values, index, axis=1)


def stretch(values):
    at = lane(values.shape)
    middle = lax.shift_right_logical(at, 1)
    beside = jnp.clip(middle + 2 * (at & 1) - 1, 0, 63)
    return 0.75 * take(values, middle) + 0.25 * take(values, beside)


def shrink(values):
    at = lane(values.shape)
    even = jnp.minimum(2 * at, 126)
    return (take(values, even) + take(values, even + 1)) * 0.125


def mix(near, far):
    return 0.75 * near + 0.25 * far


def step_kernel(
    given, faces, corners, own_tall, own, obstacle, table, around, fine_next, coarse_next, turned,
    halo, tall, blocked, rolled, coarse_blocked, fine_out, coarse_out, fine_sem, coarse_sem,
):
    def level(n, rows):
        return around[n, pl.ds(0, rows), :] == 1

    def fine_copy(i):
        return pltpu.make_async_copy(fine_out.at[pl.ds(2 * i, 2)], fine_next.at[pl.ds(2 * i, 2)], fine_sem.at[i])

    def coarse_copy():
        return pltpu.make_async_copy(coarse_out, coarse_next, coarse_sem)

    def rates(n):
        return [table[n, 0, pl.ds(q, 1), :] for q in range(27)], [table[n, 1, pl.ds(q, 1), :] for q in range(27)]

    refined = jnp.max(around[0]) == 1

    def halo_cells(side):
        dx, dy = side
        return [(2 + 2 * dx, 1 + j) if dx else (1 + j, 2 + 2 * dy) for j in range(3)]

    def received(raw):
        for slot, (dx, dy) in enumerate(CORNERS):
            both = corners[slot, pl.ds(0, 14), :]
            other = pltpu.roll(both, 64, 1)
            if raw:
                halo[2 + 2 * dx, 2 + 2 * dy, pl.ds(13, 14), :] = other
                halo[2 + 2 * dx, 2 + 2 * dy, pl.ds(0, 14), :] = both
            tall[2 + 2 * dx, 2 + 2 * dy, pl.ds(13, 14), :] = stretch(other)
            tall[2 + 2 * dx, 2 + 2 * dy, pl.ds(0, 14), :] = stretch(both)
        for slot, side in enumerate(FACES):
            spots = halo_cells(side)
            pair = faces[slot, pl.ds(0, 27), :]
            for spot, cell in zip(spots, (pair, pltpu.roll(pair, 64, 1), faces[slot, pl.ds(27, 27), :])):
                if raw:
                    halo[spot[0], spot[1], pl.ds(0, 27), :] = cell
                tall[spot[0], spot[1], pl.ds(0, 27), :] = stretch(cell)
        for i in range(3):
            for j in range(3):
                if raw:
                    halo[i + 1, j + 1, pl.ds(0, 27), pl.ds(0, 64)] = own[i, j]

    def tall_at(i, j, start, count):
        if 0 < i < 4 and 0 < j < 4:
            return own_tall[i - 1, j - 1, pl.ds(start, count), :]
        return tall[i, j, pl.ds(start, count), :]

    @pl.when(refined)
    def _():
        received(False)
        for slot, side in enumerate(FACES):
            ends = faces[slot, pl.ds(54, 9), :]
            spots = halo_cells(side)
            take_ends = level(1 + slot, 1)
            for spot, pops, rows in zip((spots[0], spots[2]), end_pops(side), (ends, pltpu.roll(ends, 64, 1))):
                rows = stretch(rows)
                for n in (0, 3, 6):
                    place = tall.at[spot[0], spot[1], pl.ds(pops[n], 3)]
                    place[...] = jnp.where(take_ends, rows[n : n + 3], place[...])
        for slot, side in enumerate(FACES):
            dx, dy = side
            pops = face_pops(side)
            edge, inner = 2 + 2 * (dx + dy), 2 + (dx + dy)
            rim = 7 if dx + dy > 0 else 0
            first, count = (pops[0], 9) if dx else (0, 27)
            if dx:
                line = [mix(tall_at(edge, j, first, count), tall_at(inner, j, first, count)) for j in range(5)]
            else:
                line = [mix(tall_at(i, edge, first, count), tall_at(i, inner, first, count)) for i in range(5)]
            cells = []
            for n in range(6):
                cells.append(mix(line[n // 2 + 1], line[n // 2 + 2 * (n % 2)]))
            turn = jnp.swapaxes(jnp.stack(cells), 0, 1)
            fine_there = level(1 + slot, 6)
            for n, q in enumerate(pops):
                values = jnp.where(fine_there, faces[slot, pl.ds(6 * n, 6), :], turn[q - first])
                if dx:
                    turned[q, rim, pl.ds(1, 6), :] = values
                else:
                    turned[q, pl.ds(1, 6), rim, :] = values

        for slot, side in enumerate(CORNERS):
            dx, dy = side
            start = corner_start(side)
            ei, ii, ej, ij = 2 + 2 * dx, 2 + dx, 2 + 2 * dy, 2 + dy
            exploded = mix(
                mix(tall_at(ei, ej, start, 3), tall_at(ii, ej, start, 3)),
                mix(tall_at(ei, ij, start, 3), tall_at(ii, ij, start, 3)),
            )
            value = jnp.where(level(5 + slot, 3), corners[slot, pl.ds(14, 3), :], exploded)
            for c in range(3):
                turned[start + c, 7 if dx > 0 else 0, pl.ds(7 if dy > 0 else 0, 1), :] = value[c : c + 1]

        blocked[...] = jnp.zeros_like(blocked)
        blocked[pl.ds(1, 6), pl.ds(1, 6), :] = obstacle[...]
        at = lane((8, 128))
        for x in range(8):
            flags = blocked[x]
            rolled[1, x] = flags
            rolled[2, x] = jnp.where(at == 0, 1, pltpu.roll(flags, 1, 1))
            rolled[0, x] = jnp.where(at == 127, 1, pltpu.roll(flags, 127, 1))

        def line(x):
            keep, pull = rates(0)
            g = []
            for q in range(27):
                ex, ey, ez = q // 9 - 1, q // 3 % 3 - 1, q % 3 - 1
                source = turned[q, x + 1 - ex, pl.ds(1 - ey, 6), :]
                if ez:
                    source = pltpu.roll(source, ez % 128, 1)
                if q == 13:
                    g.append(source)
                    continue
                stop = rolled[ez + 1, x + 1 - ex, pl.ds(1 - ey, 6), :]
                g.append(jnp.where(stop != 0, turned[26 - q, x + 1, pl.ds(1, 6), :], source))
            new = collide(g, keep, pull)
            wall = blocked[x + 1, pl.ds(1, 6), :] != 0
            new = [jnp.where(wall, turned[q, x + 1, pl.ds(1, 6), :], new[q]) for q in range(27)]
            fine_out[x] = jnp.swapaxes(jnp.stack(new), 0, 1)

        def lines(i, carry):
            line(2 * i)
            line(2 * i + 1)
            fine_copy(i).start()
            for j in range(3):
                total = (fine_out[2 * i, 2 * j] + fine_out[2 * i, 2 * j + 1]) + (
                    fine_out[2 * i + 1, 2 * j] + fine_out[2 * i + 1, 2 * j + 1]
                )
                coarse_out[i, j] = shrink(total)[:, :64]
            return carry

        lax.fori_loop(0, 3, lines, 0)
        coarse_copy().start()

    @pl.when(jnp.logical_not(refined))
    def _():
        received(True)
        for i in range(3):
            for x in (2 * i, 2 * i + 1):
                line = [mix(tall_at(i + 1, j, 0, 27), tall_at(i + 2 * (x % 2), j, 0, 27)) for j in range(5)]
                for y in range(6):
                    fine_out[x, y] = mix(line[y // 2 + 1], line[y // 2 + 2 * (y % 2)])
            fine_copy(i).start()

        keep, pull = rates(1)
        flat = turned.reshape(27 * 64, 128)
        for i in range(5):
            cells = jnp.swapaxes(halo[i, :, pl.ds(0, 27), :], 0, 1)
            for q in range(27):
                flat[pl.ds(64 * q + 5 * i, 5), :] = cells[q]
        column = jnp.maximum(
            jnp.maximum(obstacle[2, pl.ds(2, 1), :], obstacle[2, pl.ds(3, 1), :]),
            jnp.maximum(obstacle[3, pl.ds(2, 1), :], obstacle[3, pl.ds(3, 1), :]),
        )
        wide = jnp.broadcast_to(column, (8, 128))
        at = lane((8, 128))
        even = jnp.minimum(2 * at, 126)
        flags = jnp.maximum(take(wide, even), take(wide, even + 1))
        flags = jnp.where(at < 64, flags, 0)
        coarse_blocked[...] = jnp.zeros_like(coarse_blocked)
        coarse_blocked[1, pl.ds(12, 1), :] = flags[:1]
        high = lane((32, 128))
        coarse_blocked[2] = jnp.where(high == 0, 1, pltpu.roll(coarse_blocked[1], 1, 1))
        coarse_blocked[0] = jnp.where(high == 63, 1, pltpu.roll(coarse_blocked[1], 127, 1))
        g = []
        for q in range(27):
            ex, ey, ez = q // 9 - 1, q // 3 % 3 - 1, q % 3 - 1
            start = 6 - 5 * ex - ey
            source = flat[pl.ds(64 * q + start, 13), :]
            if ez:
                source = pltpu.roll(source, ez % 128, 1)
            if q != 13:
                stop = coarse_blocked[ez + 1, pl.ds(start, 13), :]
                source = jnp.where(stop != 0, flat[pl.ds(64 * (26 - q) + 6, 13), :], source)
            g.append(source)
        new = collide(g, keep, pull)
        wall = coarse_blocked[1, pl.ds(6, 13), :] != 0
        new = [jnp.where(wall, flat[pl.ds(64 * q + 6, 13), :], new[q]) for q in range(27)]
        turn = jnp.swapaxes(jnp.stack(new), 0, 1)
        for i in range(3):
            for j in range(3):
                coarse_out[i, j] = turn[5 * i + j][:, :64]
        coarse_copy().start()

    for i in range(3):
        fine_copy(i).wait()
    coarse_copy().wait()


def step(*args):
    vmem = pl.BlockSpec(memory_space=pltpu.VMEM)
    hbm = pl.BlockSpec(memory_space=pltpu.HBM)
    return pl.pallas_call(
        step_kernel,
        out_shape=(
            jax.ShapeDtypeStruct((6, 6, 27, 128), F32),
            jax.ShapeDtypeStruct((3, 3, 27, 64), F32),
            jax.ShapeDtypeStruct((27, 8, 8, 128), F32),
        ),
        in_specs=[vmem] * 8,
        out_specs=(hbm, hbm, vmem),
        input_output_aliases={0: 2},
        scratch_shapes=[
            pltpu.VMEM((5, 5, 32, 128), F32),
            pltpu.VMEM((5, 5, 32, 128), F32),
            pltpu.VMEM((8, 8, 128), jnp.int32),
            pltpu.VMEM((3, 8, 8, 128), jnp.int32),
            pltpu.VMEM((3, 32, 128), jnp.int32),
            pltpu.VMEM((6, 6, 27, 128), F32),
            pltpu.VMEM((3, 3, 27, 64), F32),
            pltpu.SemaphoreType.DMA((3,)),
            pltpu.SemaphoreType.DMA,
        ],
        compiler_params=pltpu.CompilerParams(vmem_limit_bytes=24 * 2**20),
    )(*args)


def solution(mesh):
    n_stream, n_span = mesh.shape["stream"], mesh.shape["span"]

    def local(fine_pops, coarse_pops, obstacle, block_level, relax_rates):
        fine = jnp.transpose(fine_pops, (1, 2, 0, 3))
        coarse = jnp.transpose(coarse_pops, (1, 2, 0, 3))
        ready = exchange(n_stream, n_span, fine, coarse, obstacle, block_level, relax_rates)
        fine_next, coarse_next, _ = step(*ready)
        return jnp.transpose(fine_next, (2, 0, 1, 3)), jnp.transpose(coarse_next, (2, 0, 1, 3))

    placed = P(None, "stream", "span", None)
    return jax.shard_map(
        local,
        mesh=mesh,
        in_specs=(placed, placed, P("stream", "span", None), P(), P()),
        out_specs=(placed, placed),
        check_vma=False,
    )
```

```python
import functools

import jax
import jax.numpy as jnp
from jax import lax
from jax.experimental import pallas as pl
from jax.experimental.pallas import tpu as pltpu
from jax.sharding import PartitionSpec as P

MESH = pl.DeviceIdType.MESH
F32 = jnp.float32
FACES = ((-1, 0), (1, 0), (0, -1), (0, 1))
CORNERS = ((-1, -1), (-1, 1), (1, -1), (1, 1))


def face_pops(side):
    dx, dy = side
    return [q for q in range(27) if (q // 9 - 1 == -dx if dx else q // 3 % 3 - 1 == -dy)]


def corner_start(side):
    dx, dy = side
    return 9 * (1 - dx) + 3 * (1 - dy)


def face_cells(side):
    dx, dy = side
    return [(1 - dx, j) for j in range(3)] if dx else [(i, 1 - dy) for i in range(3)]


def end_pops(side):
    dx, dy = side
    return [face_pops((0, s) if dx else (s, 0)) for s in (-1, 1)]


def pick_rows(cell, pops):
    return jnp.concatenate([cell[q : q + 3] for q in pops[::3]], axis=0)


def rates_of(table, n):
    return [table[n, 0, pl.ds(q, 1), :] for q in range(27)], [table[n, 1, pl.ds(q, 1), :] for q in range(27)]


def exchange_kernel(
    n_stream, n_span, fine, coarse, obstacle, level, rates,
    turned, faces, corners, tall, own, inner, coarse_stop, table, around,
    native, flags, levels, speeds, blocked, rolled, face_out, corner_out, load_sem, send_sem, recv_sem,
):
    row, col = lax.axis_index("stream"), lax.axis_index("span")

    def at(side):
        return (lax.rem(row + side[0] + n_stream, n_stream), lax.rem(col + side[1] + n_span, n_span))

    barrier = pltpu.get_barrier_semaphore()
    loads = [
        pltpu.make_async_copy(fine, native, load_sem.at[0]),
        pltpu.make_async_copy(coarse, own, load_sem.at[1]),
        pltpu.make_async_copy(level, levels, load_sem.at[2]),
        pltpu.make_async_copy(obstacle, flags, load_sem.at[3]),
        pltpu.make_async_copy(rates, speeds, load_sem.at[4]),
    ]
    for load in loads:
        load.start()
    for side in CORNERS + FACES:
        pl.semaphore_signal(barrier, inc=1, device_id=at(side), device_id_type=MESH)
    for load in loads[:3]:
        load.wait()
    here = levels[row, col]
    there = [levels[at(side)[0], at(side)[1]] for side in FACES + CORNERS]
    for slot, side in enumerate(CORNERS):
        dx, dy = side
        cell = own[1 - dx, 1 - dy]
        corner_out[slot, pl.ds(0, 14), :] = jnp.concatenate([cell[0:14], cell[13:27]], axis=1)
        corner_out[slot, pl.ds(14, 3), :] = native[
            5 if dx < 0 else 0, 5 if dy < 0 else 0, pl.ds(corner_start(side), 3), :
        ]
    for slot, side in enumerate(FACES):
        dx, dy = side
        both = (here == 1) & (there[FACES.index((-dx, -dy))] == 1)
        cells = [own[i, j] for i, j in face_cells(side)]
        face_out[slot, pl.ds(0, 27), :] = jnp.concatenate([cells[0], cells[1]], axis=1)
        face_out[slot, pl.ds(27, 27), :] = jnp.concatenate([cells[2], cells[2]], axis=1)
        edge = native[5 if dx < 0 else 0] if dx else native[:, 5 if dy < 0 else 0]
        edge = jnp.swapaxes(edge, 0, 1)
        for n, q in enumerate(face_pops(side)):
            spot = face_out.at[slot, pl.ds(6 * n, 6)]
            spot[...] = jnp.where(both, edge[q], spot[...])
        ends = [pick_rows(cell, pops) for cell, pops in zip((cells[0], cells[2]), end_pops(side))]
        face_out[slot, pl.ds(54, 9), :] = jnp.concatenate(ends, axis=1)
    pl.semaphore_wait(barrier, 8)
    copies = []
    for slot, (dx, dy) in enumerate(CORNERS):
        copies.append(
            pltpu.make_async_remote_copy(
                corner_out.at[slot, pl.ds(0, 17)], corners.at[slot, pl.ds(0, 17)],
                send_sem.at[4 + slot], recv_sem.at[4 + slot], device_id=at((-dx, -dy)), device_id_type=MESH,
            )
        )
    for slot, (dx, dy) in enumerate(FACES):
        copies.append(
            pltpu.make_async_remote_copy(
                face_out.at[slot, pl.ds(0, 63)], faces.at[slot, pl.ds(0, 63)],
                send_sem.at[slot], recv_sem.at[slot], device_id=at((-dx, -dy)), device_id_type=MESH,
            )
        )
    for copy in copies:
        copy.start()
    for x in range(6):
        turned[:, x + 1, pl.ds(1, 6), :] = jnp.swapaxes(native[x], 0, 1)
    for i in range(3):
        for j in range(3):
            cell = own[i, j]
            tall[i, j] = stretch(jnp.concatenate([cell, cell], axis=1))
    for n, value in enumerate([here] + there):
        around[n] = jnp.full((8, 128), value, jnp.int32)
    for load in loads[3:]:
        load.wait()
    for q in range(27):
        orders = (q // 9, q // 3 % 3, q % 3)
        share = 0.0 if 1 in orders else 0.125 / 3.0 ** orders.count(2)
        fine_rate = jnp.full((1, 128), speeds[q], F32)
        for n, rate in enumerate((fine_rate, 1.0 / (2.0 / fine_rate - 0.5))):
            table[n, 0, pl.ds(q, 1), :] = (1.0 - rate) * 0.125
            table[n, 1, pl.ds(q, 1), :] = rate * share
    blocked[...] = jnp.zeros_like(blocked)
    blocked[pl.ds(1, 6), pl.ds(1, 6), :] = flags[...]
    rows = lane((8, 128))
    for x in range(8):
        stop = blocked[x]
        rolled[1, x] = stop
        rolled[2, x] = jnp.where(rows == 0, 1, pltpu.roll(stop, 1, 1))
        rolled[0, x] = jnp.where(rows == 127, 1, pltpu.roll(stop, 127, 1))
    stop = jnp.maximum(jnp.maximum(blocked[3], blocked[4]), pltpu.roll(jnp.maximum(blocked[3], blocked[4]), 7, 0))
    even = jnp.minimum(2 * rows, 126)
    stop = jnp.where(rows < 64, jnp.maximum(take(stop, even), take(stop, even + 1)), 0)
    coarse_stop[...] = jnp.zeros_like(coarse_stop)
    coarse_stop[1, pl.ds(12, 1), :] = stop[3:4]
    high = lane((32, 128))
    coarse_stop[2] = jnp.where(high == 0, 1, pltpu.roll(coarse_stop[1], 1, 1))
    coarse_stop[0] = jnp.where(high == 63, 1, pltpu.roll(coarse_stop[1], 127, 1))

    def middle(x, carry):
        keep, pull = rates_of(table, 0)
        g = []
        for q in range(27):
            ex, ey, ez = q // 9 - 1, q // 3 % 3 - 1, q % 3 - 1
            source = turned[q, x + 1 - ex, pl.ds(1 - ey, 6), :]
            if ez:
                source = pltpu.roll(source, ez % 128, 1)
            if q != 13:
                stop = rolled[ez + 1, x + 1 - ex, pl.ds(1 - ey, 6), :]
                source = jnp.where(stop != 0, turned[26 - q, x + 1, pl.ds(1, 6), :], source)
            g.append(source)
        new = collide(g, keep, pull)
        wall = blocked[x + 1, pl.ds(1, 6), :] != 0
        new = [jnp.where(wall, turned[q, x + 1, pl.ds(1, 6), :], new[q]) for q in range(27)]
        inner[x - 1] = jnp.swapaxes(jnp.stack(new), 0, 1)[1:5]
        return carry

    lax.fori_loop(1, 5, middle, 0)
    for x in range(1, 5):
        line = [mix(tall[x // 2, j], tall[x // 2 - 1 + 2 * (x % 2), j]) for j in range(3)]
        for y in range(1, 5):
            exploded = mix(line[y // 2], line[y // 2 - 1 + 2 * (y % 2)])
            inner[x - 1, y - 1] = jnp.where(here == 1, inner[x - 1, y - 1], exploded)
    for copy in copies:
        copy.wait()


def exchange(n_stream, n_span, *args):
    hbm = pl.BlockSpec(memory_space=pltpu.HBM)
    vmem = pl.BlockSpec(memory_space=pltpu.VMEM)
    return pl.pallas_call(
        functools.partial(exchange_kernel, n_stream, n_span),
        out_shape=(
            jax.ShapeDtypeStruct((27, 8, 8, 128), F32),
            jax.ShapeDtypeStruct((4, 64, 128), F32),
            jax.ShapeDtypeStruct((4, 24, 128), F32),
            jax.ShapeDtypeStruct((3, 3, 27, 128), F32),
            jax.ShapeDtypeStruct((3, 3, 27, 64), F32),
            jax.ShapeDtypeStruct((4, 4, 27, 128), F32),
            jax.ShapeDtypeStruct((3, 32, 128), jnp.int32),
            jax.ShapeDtypeStruct((2, 2, 32, 128), F32),
            jax.ShapeDtypeStruct((9, 8, 128), jnp.int32),
        ),
        in_specs=[hbm] * 5,
        out_specs=(vmem,) * 9,
        scratch_shapes=[
            pltpu.VMEM((6, 6, 27, 128), F32),
            pltpu.VMEM((6, 6, 128), jnp.int32),
            pltpu.SMEM((16, 32), jnp.int32),
            pltpu.SMEM((27,), F32),
            pltpu.VMEM((8, 8, 128), jnp.int32),
            pltpu.VMEM((3, 8, 8, 128), jnp.int32),
            pltpu.VMEM((4, 64, 128), F32),
            pltpu.VMEM((4, 24, 128), F32),
            pltpu.SemaphoreType.DMA((5,)),
            pltpu.SemaphoreType.DMA((8,)),
            pltpu.SemaphoreType.DMA((8,)),
        ],
        compiler_params=pltpu.CompilerParams(
            collective_id=0, has_side_effects=True, vmem_limit_bytes=24 * 2**20
        ),
    )(*[pltpu.with_memory_space_constraint(arg, pltpu.HBM) for arg in args])


def forward(low, mid, high, speed, total=None):
    pair, diff = high + low, high - low
    if total is None:
        total = pair + 4.0 * mid
    first = diff - speed * total
    return total, first, pair - speed * (diff + first)


def backward(total, first, second, speed):
    slope = first + speed * total
    curve = second + speed * (first + slope)
    return curve - slope, 0.5 * (total - curve), curve + slope


def collide(g, keep, pull):
    t0 = [g[r] + g[18 + r] + 4.0 * g[9 + r] for r in range(9)]
    dx = [g[18 + r] - g[r] for r in range(9)]
    s0 = [t0[c] + t0[6 + c] + 4.0 * t0[3 + c] for c in range(3)]
    dy = [t0[6 + c] - t0[c] for c in range(3)]
    density = s0[0] + s0[2] + 4.0 * s0[1]
    ex = [dx[c] + dx[6 + c] + 4.0 * dx[3 + c] for c in range(3)]
    inverse = 1.0 / density
    ux = (ex[0] + ex[2] + 4.0 * ex[1]) * inverse
    uy = (dy[0] + dy[2] + 4.0 * dy[1]) * inverse
    uz = (s0[2] - s0[0]) * inverse
    k = [None] * 27
    for r in range(9):
        k[r], k[9 + r], k[18 + r] = forward(g[r], g[9 + r], g[18 + r], ux, t0[r])
    for a in range(3):
        for c in range(3):
            i = 9 * a + c
            k[i], k[i + 3], k[i + 6] = forward(k[i], k[i + 3], k[i + 6], uy, s0[c] if a == 0 else None)
    for i in range(0, 27, 3):
        k[i], k[i + 1], k[i + 2] = forward(k[i], k[i + 1], k[i + 2], uz, density if i == 0 else None)
    for q in range(27):
        k[q] = keep[q] * k[q] if 1 in (q // 9, q // 3 % 3, q % 3) else keep[q] * k[q] + pull[q] * density
    for i in range(0, 27, 3):
        k[i], k[i + 1], k[i + 2] = backward(k[i], k[i + 1], k[i + 2], uz)
    for a in range(3):
        for c in range(3):
            i = 9 * a + c
            k[i], k[i + 3], k[i + 6] = backward(k[i], k[i + 3], k[i + 6], uy)
    for r in range(9):
        k[r], k[9 + r], k[18 + r] = backward(k[r], k[9 + r], k[18 + r], ux)
    return k


def lane(shape):
    return lax.broadcasted_iota(jnp.int32, shape, len(shape) - 1)


def take(values, index):
    return jnp.take_along_axis(values, index, axis=1)


def stretch(values):
    at = lane(values.shape)
    middle = lax.shift_right_logical(at, 1)
    beside = jnp.clip(middle + 2 * (at & 1) - 1, 0, 63)
    return 0.75 * take(values, middle) + 0.25 * take(values, beside)


def shrink(values):
    at = lane(values.shape)
    even = jnp.minimum(2 * at, 126)
    return (take(values, even) + take(values, even + 1)) * 0.125


def mix(near, far):
    return 0.75 * near + 0.25 * far


def step_kernel(
    given, faces, corners, own_tall, own, inner, coarse_stop, table, around, fine_next, coarse_next, turned,
    halo, tall, edge_x, edge_y, coarse_out, sems,
):
    inner_copy = pltpu.make_async_copy(inner, fine_next.at[pl.ds(1, 4), pl.ds(1, 4)], sems.at[0])
    inner_copy.start()
    x_copies = [pltpu.make_async_copy(edge_x.at[n], fine_next.at[5 * n], sems.at[1 + n]) for n in range(2)]
    y_copies = [
        pltpu.make_async_copy(edge_y.at[n], fine_next.at[pl.ds(1, 4), 5 * n], sems.at[3 + n]) for n in range(2)
    ]
    coarse_copy = pltpu.make_async_copy(coarse_out, coarse_next, sems.at[5])

    def level(n, rows):
        return around[n, pl.ds(0, rows), :] == 1

    def cell(x, y):
        if x % 5 == 0:
            return edge_x[x // 5, y]
        if y % 5 == 0:
            return edge_y[y // 5, x - 1]
        return inner[x - 1, y - 1]

    refined = jnp.max(around[0]) == 1

    def halo_cells(side):
        dx, dy = side
        return [(2 + 2 * dx, 1 + j) if dx else (1 + j, 2 + 2 * dy) for j in range(3)]

    def received(raw):
        for slot, (dx, dy) in enumerate(CORNERS):
            both = corners[slot, pl.ds(0, 14), :]
            other = pltpu.roll(both, 64, 1)
            if raw:
                halo[2 + 2 * dx, 2 + 2 * dy, pl.ds(13, 14), :] = other
                halo[2 + 2 * dx, 2 + 2 * dy, pl.ds(0, 14), :] = both
            tall[2 + 2 * dx, 2 + 2 * dy, pl.ds(13, 14), :] = stretch(other)
            tall[2 + 2 * dx, 2 + 2 * dy, pl.ds(0, 14), :] = stretch(both)
        for slot, side in enumerate(FACES):
            spots = halo_cells(side)
            pair = faces[slot, pl.ds(0, 27), :]
            for spot, cell in zip(spots, (pair, pltpu.roll(pair, 64, 1), faces[slot, pl.ds(27, 27), :])):
                if raw:
                    halo[spot[0], spot[1], pl.ds(0, 27), :] = cell
                tall[spot[0], spot[1], pl.ds(0, 27), :] = stretch(cell)
        for i in range(3):
            for j in range(3):
                if raw:
                    halo[i + 1, j + 1, pl.ds(0, 27), pl.ds(0, 64)] = own[i, j]

    def tall_at(i, j, start, count):
        if 0 < i < 4 and 0 < j < 4:
            return own_tall[i - 1, j - 1, pl.ds(start, count), :]
        return tall[i, j, pl.ds(start, count), :]

    @pl.when(refined)
    def _():
        received(False)
        for slot, side in enumerate(FACES):
            ends = faces[slot, pl.ds(54, 9), :]
            spots = halo_cells(side)
            take_ends = level(1 + slot, 1)
            for spot, pops, rows in zip((spots[0], spots[2]), end_pops(side), (ends, pltpu.roll(ends, 64, 1))):
                rows = stretch(rows)
                for n in (0, 3, 6):
                    place = tall.at[spot[0], spot[1], pl.ds(pops[n], 3)]
                    place[...] = jnp.where(take_ends, rows[n : n + 3], place[...])
        for slot, side in enumerate(FACES):
            dx, dy = side
            pops = face_pops(side)
            edge, inner = 2 + 2 * (dx + dy), 2 + (dx + dy)
            rim = 7 if dx + dy > 0 else 0
            first, count = (pops[0], 9) if dx else (0, 27)
            if dx:
                line = [mix(tall_at(edge, j, first, count), tall_at(inner, j, first, count)) for j in range(5)]
            else:
                line = [mix(tall_at(i, edge, first, count), tall_at(i, inner, first, count)) for i in range(5)]
            cells = []
            for n in range(6):
                cells.append(mix(line[n // 2 + 1], line[n // 2 + 2 * (n % 2)]))
            turn = jnp.swapaxes(jnp.stack(cells), 0, 1)
            fine_there = level(1 + slot, 6)
            for n, q in enumerate(pops):
                values = jnp.where(fine_there, faces[slot, pl.ds(6 * n, 6), :], turn[q - first])
                if dx:
                    turned[q, rim, pl.ds(1, 6), :] = values
                else:
                    turned[q, pl.ds(1, 6), rim, :] = values

        for slot, side in enumerate(CORNERS):
            dx, dy = side
            start = corner_start(side)
            ei, ii, ej, ij = 2 + 2 * dx, 2 + dx, 2 + 2 * dy, 2 + dy
            exploded = mix(
                mix(tall_at(ei, ej, start, 3), tall_at(ii, ej, start, 3)),
                mix(tall_at(ei, ij, start, 3), tall_at(ii, ij, start, 3)),
            )
            value = jnp.where(level(5 + slot, 3), corners[slot, pl.ds(14, 3), :], exploded)
            for c in range(3):
                turned[start + c, 7 if dx > 0 else 0, pl.ds(7 if dy > 0 else 0, 1), :] = value[c : c + 1]

        keep, pull = rates_of(table, 0)

        def advance(load, count):
            at = lane((count, 128))
            still = [load(q, 0, 0) for q in range(27)]
            g = []
            for q in range(27):
                ex, ey, ez = q // 9 - 1, q // 3 % 3 - 1, q % 3 - 1
                source = load(q, ex, ey) if ex or ey else still[q]
                if ez:
                    source = jnp.where(at == (0 if ez > 0 else 127), still[26 - q], pltpu.roll(source, ez % 128, 1))
                g.append(source)
            return jnp.swapaxes(jnp.stack(collide(g, keep, pull)), 0, 1)

        for n in range(2):
            edge_x[n] = advance(lambda q, ex, ey: turned[q, 5 * n + 1 - ex, pl.ds(1 - ey, 6), :], 6)
            x_copies[n].start()
        both = advance(
            lambda q, ex, ey: jnp.concatenate(
                [turned[q, pl.ds(2 - ex, 4), 1 - ey, :], turned[q, pl.ds(2 - ex, 4), 6 - ey, :]], axis=0
            ),
            8,
        )
        for n in range(2):
            edge_y[n] = both[4 * n : 4 * n + 4]
            y_copies[n].start()
        for i in range(3):
            for j in range(3):
                total = (cell(2 * i, 2 * j) + cell(2 * i, 2 * j + 1)) + (
                    cell(2 * i + 1, 2 * j) + cell(2 * i + 1, 2 * j + 1)
                )
                coarse_out[i, j] = shrink(total)[:, :64]
        coarse_copy.start()

    @pl.when(jnp.logical_not(refined))
    def _():
        received(True)
        for x in range(6):
            line = [mix(tall_at(x // 2 + 1, j, 0, 27), tall_at(x // 2 + 2 * (x % 2), j, 0, 27)) for j in range(5)]
            for y in range(6) if x % 5 == 0 else (0, 5):
                exploded = mix(line[y // 2 + 1], line[y // 2 + 2 * (y % 2)])
                if x % 5 == 0:
                    edge_x[x // 5, y] = exploded
                else:
                    edge_y[y // 5, x - 1] = exploded
            if x % 5 == 0:
                x_copies[x // 5].start()
        for n in range(2):
            y_copies[n].start()

        keep, pull = rates_of(table, 1)
        flat = turned.reshape(27 * 64, 128)
        for i in range(5):
            cells = jnp.swapaxes(halo[i, :, pl.ds(0, 27), :], 0, 1)
            for q in range(27):
                flat[pl.ds(64 * q + 5 * i, 5), :] = cells[q]
        g = []
        for q in range(27):
            ex, ey, ez = q // 9 - 1, q // 3 % 3 - 1, q % 3 - 1
            start = 6 - 5 * ex - ey
            source = flat[pl.ds(64 * q + start, 13), :]
            if ez:
                source = pltpu.roll(source, ez % 128, 1)
            if q != 13:
                stop = coarse_stop[ez + 1, pl.ds(start, 13), :]
                source = jnp.where(stop != 0, flat[pl.ds(64 * (26 - q) + 6, 13), :], source)
            g.append(source)
        new = collide(g, keep, pull)
        wall = coarse_stop[1, pl.ds(6, 13), :] != 0
        new = [jnp.where(wall, flat[pl.ds(64 * q + 6, 13), :], new[q]) for q in range(27)]
        turn = jnp.swapaxes(jnp.stack(new), 0, 1)
        for i in range(3):
            for j in range(3):
                coarse_out[i, j] = turn[5 * i + j][:, :64]
        coarse_copy.start()

    for copy in [inner_copy, coarse_copy] + x_copies + y_copies:
        copy.wait()


def step(*args):
    vmem = pl.BlockSpec(memory_space=pltpu.VMEM)
    hbm = pl.BlockSpec(memory_space=pltpu.HBM)
    return pl.pallas_call(
        step_kernel,
        out_shape=(
            jax.ShapeDtypeStruct((6, 6, 27, 128), F32),
            jax.ShapeDtypeStruct((3, 3, 27, 64), F32),
            jax.ShapeDtypeStruct((27, 8, 8, 128), F32),
        ),
        in_specs=[vmem] * 9,
        out_specs=(hbm, hbm, vmem),
        input_output_aliases={0: 2},
        scratch_shapes=[
            pltpu.VMEM((5, 5, 32, 128), F32),
            pltpu.VMEM((5, 5, 32, 128), F32),
            pltpu.VMEM((2, 6, 27, 128), F32),
            pltpu.VMEM((2, 4, 27, 128), F32),
            pltpu.VMEM((3, 3, 27, 64), F32),
            pltpu.SemaphoreType.DMA((6,)),
        ],
        compiler_params=pltpu.CompilerParams(vmem_limit_bytes=24 * 2**20),
    )(*args)


def solution(mesh):
    n_stream, n_span = mesh.shape["stream"], mesh.shape["span"]

    def local(fine_pops, coarse_pops, obstacle, block_level, relax_rates):
        fine = jnp.transpose(fine_pops, (1, 2, 0, 3))
        coarse = jnp.transpose(coarse_pops, (1, 2, 0, 3))
        ready = exchange(n_stream, n_span, fine, coarse, obstacle, block_level, relax_rates)
        fine_next, coarse_next, _ = step(*ready)
        return jnp.transpose(fine_next, (2, 0, 1, 3)), jnp.transpose(coarse_next, (2, 0, 1, 3))

    placed = P(None, "stream", "span", None)
    return jax.shard_map(
        local,
        mesh=mesh,
        in_specs=(placed, placed, P("stream", "span", None), P(), P()),
        out_specs=(placed, placed),
        check_vma=False,
    )
```

```python
import functools

import jax
import jax.numpy as jnp
from jax import lax
from jax.experimental import pallas as pl
from jax.experimental.pallas import tpu as pltpu
from jax.sharding import PartitionSpec as P

MESH = pl.DeviceIdType.MESH
F32 = jnp.float32
FACES = ((-1, 0), (1, 0), (0, -1), (0, 1))
CORNERS = ((-1, -1), (-1, 1), (1, -1), (1, 1))


def face_pops(side):
    dx, dy = side
    return [q for q in range(27) if (q // 9 - 1 == -dx if dx else q // 3 % 3 - 1 == -dy)]


def corner_start(side):
    dx, dy = side
    return 9 * (1 - dx) + 3 * (1 - dy)


def face_cells(side):
    dx, dy = side
    return [(1 - dx, j) for j in range(3)] if dx else [(i, 1 - dy) for i in range(3)]


def halo_cells(side):
    dx, dy = side
    return [(2 + 2 * dx, 1 + j) if dx else (1 + j, 2 + 2 * dy) for j in range(3)]


def end_pops(side):
    dx, dy = side
    return [face_pops((0, s) if dx else (s, 0)) for s in (-1, 1)]


def pick_rows(cell, pops):
    return jnp.concatenate([cell[q : q + 3] for q in pops[::3]], axis=0)


def rates_of(table, n):
    return [table[n, 0, pl.ds(q, 1), :] for q in range(27)], [table[n, 1, pl.ds(q, 1), :] for q in range(27)]


def unfold(raw, tall, fold):
    raw[pl.ds(0, 16), :] = fold
    raw[pl.ds(16, 16), :] = pltpu.roll(fold, 64, 1)
    tall[pl.ds(0, 16), :] = stretch(fold)
    tall[pl.ds(16, 16), :] = stretch(fold, 1)


def exchange_kernel(
    n_stream, n_span, fine, coarse, obstacle, level, rates,
    turned, faces, corners, halo, tall, inner, coarse_stop, table, around,
    native, own, flags, levels, speeds, blocked, rolled, face_out, corner_out, load_sem, send_sem, recv_sem,
):
    row, col = lax.axis_index("stream"), lax.axis_index("span")

    def at(side):
        return (lax.rem(row + side[0] + n_stream, n_stream), lax.rem(col + side[1] + n_span, n_span))

    barrier = pltpu.get_barrier_semaphore()
    for i in range(3):
        for j in range(3):
            own[i, j, pl.ds(24, 8), :] = jnp.zeros((8, 64), F32)
    loads = [
        pltpu.make_async_copy(fine, native, load_sem.at[0]),
        pltpu.make_async_copy(coarse, own.at[:, :, pl.ds(0, 27)], load_sem.at[1]),
        pltpu.make_async_copy(level, levels, load_sem.at[2]),
        pltpu.make_async_copy(obstacle, flags, load_sem.at[3]),
        pltpu.make_async_copy(rates, speeds, load_sem.at[4]),
    ]
    for load in loads:
        load.start()
    for side in CORNERS + FACES:
        pl.semaphore_signal(barrier, inc=1, device_id=at(side), device_id_type=MESH)
    for load in loads[:3]:
        load.wait()
    here = levels[row, col]
    there = [levels[at(side)[0], at(side)[1]] for side in FACES + CORNERS]
    for slot, side in enumerate(CORNERS):
        dx, dy = side
        cell = own[1 - dx, 1 - dy]
        corner_out[slot, pl.ds(0, 16), :] = jnp.concatenate([cell[0:16], cell[16:32]], axis=1)
        corner_out[slot, pl.ds(16, 3), :] = native[
            5 if dx < 0 else 0, 5 if dy < 0 else 0, pl.ds(corner_start(side), 3), :
        ]
    for slot, side in enumerate(FACES):
        dx, dy = side
        both = (here == 1) & (there[FACES.index((-dx, -dy))] == 1)
        cells = [own[i, j] for i, j in face_cells(side)]
        face_out[slot, pl.ds(0, 32), :] = jnp.concatenate([cells[0], cells[1]], axis=1)
        face_out[slot, pl.ds(32, 16), :] = jnp.concatenate([cells[2][0:16], cells[2][16:32]], axis=1)
        face_out[slot, pl.ds(48, 8), :] = jnp.zeros((8, 128), F32)
        edge = native[5 if dx < 0 else 0] if dx else native[:, 5 if dy < 0 else 0]
        edge = jnp.swapaxes(edge, 0, 1)
        for n, q in enumerate(face_pops(side)):
            spot = face_out.at[slot, pl.ds(6 * n, 6)]
            spot[...] = jnp.where(both, edge[q], spot[...])
        ends = [pick_rows(cell, pops) for cell, pops in zip((cells[0], cells[2]), end_pops(side))]
        face_out[slot, pl.ds(56, 9), :] = jnp.concatenate(ends, axis=1)
    pl.semaphore_wait(barrier, 8)
    copies = []
    for slot, (dx, dy) in enumerate(CORNERS):
        copies.append(
            pltpu.make_async_remote_copy(
                corner_out.at[slot, pl.ds(0, 19)], corners.at[slot, pl.ds(0, 19)],
                send_sem.at[4 + slot], recv_sem.at[4 + slot], device_id=at((-dx, -dy)), device_id_type=MESH,
            )
        )
    for slot, (dx, dy) in enumerate(FACES):
        copies.append(
            pltpu.make_async_remote_copy(
                face_out.at[slot, pl.ds(0, 65)], faces.at[slot, pl.ds(0, 65)],
                send_sem.at[slot], recv_sem.at[slot], device_id=at((-dx, -dy)), device_id_type=MESH,
            )
        )
    for copy in copies:
        copy.start()
    for x in range(6):
        turned[:, x + 1, pl.ds(1, 6), :] = jnp.swapaxes(native[x], 0, 1)
    for i in range(3):
        for j in range(3):
            cell = own[i, j]
            halo[i + 1, j + 1, :, pl.ds(0, 64)] = cell
            tall[i + 1, j + 1] = stretch(jnp.concatenate([cell, cell], axis=1))
    for n, value in enumerate([here] + there):
        around[n] = jnp.full((8, 128), value, jnp.int32)
    for load in loads[3:]:
        load.wait()
    for q in range(27):
        orders = (q // 9, q // 3 % 3, q % 3)
        share = 0.0 if 1 in orders else 0.125 / 3.0 ** orders.count(2)
        fine_rate = jnp.full((1, 128), speeds[q], F32)
        for n, rate in enumerate((fine_rate, 1.0 / (2.0 / fine_rate - 0.5))):
            table[n, 0, pl.ds(q, 1), :] = (1.0 - rate) * 0.125
            table[n, 1, pl.ds(q, 1), :] = rate * share
    blocked[...] = jnp.zeros_like(blocked)
    blocked[pl.ds(1, 6), pl.ds(1, 6), :] = flags[...]
    rows = lane((8, 128))
    for x in range(8):
        stop = blocked[x]
        rolled[1, x] = stop
        rolled[2, x] = jnp.where(rows == 0, 1, pltpu.roll(stop, 1, 1))
        rolled[0, x] = jnp.where(rows == 127, 1, pltpu.roll(stop, 127, 1))
    stop = jnp.maximum(jnp.maximum(blocked[3], blocked[4]), pltpu.roll(jnp.maximum(blocked[3], blocked[4]), 7, 0))
    even = jnp.minimum(2 * rows, 126)
    stop = jnp.where(rows < 64, jnp.maximum(take(stop, even), take(stop, even + 1)), 0)
    coarse_stop[...] = jnp.zeros_like(coarse_stop)
    coarse_stop[1, pl.ds(12, 1), :] = stop[3:4]
    high = lane((32, 128))
    coarse_stop[2] = jnp.where(high == 0, 1, pltpu.roll(coarse_stop[1], 1, 1))
    coarse_stop[0] = jnp.where(high == 63, 1, pltpu.roll(coarse_stop[1], 127, 1))

    def middle(x, carry):
        keep, pull = rates_of(table, 0)
        g = []
        for q in range(27):
            ex, ey, ez = q // 9 - 1, q // 3 % 3 - 1, q % 3 - 1
            source = turned[q, x + 1 - ex, pl.ds(1 - ey, 6), :]
            if ez:
                source = pltpu.roll(source, ez % 128, 1)
            if q != 13:
                stop = rolled[ez + 1, x + 1 - ex, pl.ds(1 - ey, 6), :]
                source = jnp.where(stop != 0, turned[26 - q, x + 1, pl.ds(1, 6), :], source)
            g.append(source)
        new = collide(g, keep, pull)
        wall = blocked[x + 1, pl.ds(1, 6), :] != 0
        new = [jnp.where(wall, turned[q, x + 1, pl.ds(1, 6), :], new[q]) for q in range(27)]
        inner[x - 1] = jnp.swapaxes(jnp.stack(new), 0, 1)[1:5]
        return carry

    lax.fori_loop(1, 5, middle, 0)
    for x in range(1, 5):
        line = [mix(tall[x // 2 + 1, j, pl.ds(0, 27), :], tall[x // 2 + 2 * (x % 2), j, pl.ds(0, 27), :]) for j in (1, 2, 3)]
        for y in range(1, 5):
            exploded = mix(line[y // 2], line[y // 2 - 1 + 2 * (y % 2)])
            inner[x - 1, y - 1] = jnp.where(here == 1, inner[x - 1, y - 1], exploded)
    for slot, side in enumerate(FACES):
        copies[4 + slot].wait()
        pair, fold = faces[slot, pl.ds(0, 32), :], faces[slot, pl.ds(32, 16), :]
        spots = halo_cells(side)
        halo[spots[0][0], spots[0][1]] = pair
        halo[spots[1][0], spots[1][1]] = pltpu.roll(pair, 64, 1)
        tall[spots[0][0], spots[0][1]] = stretch(pair)
        tall[spots[1][0], spots[1][1]] = stretch(pair, 1)
        unfold(halo.at[spots[2][0], spots[2][1]], tall.at[spots[2][0], spots[2][1]], fold)
        both = (here == 1) & (there[slot] == 1)
        ends = faces[slot, pl.ds(56, 9), :]
        for half, (spot, pops) in enumerate(zip((spots[0], spots[2]), end_pops(side))):
            rows = stretch(ends, half)
            for n in (0, 3, 6):
                place = tall.at[spot[0], spot[1], pl.ds(pops[n], 3)]
                place[...] = jnp.where(both, rows[n : n + 3], place[...])
    for copy in copies[:4]:
        copy.wait()


def exchange(n_stream, n_span, *args):
    hbm = pl.BlockSpec(memory_space=pltpu.HBM)
    vmem = pl.BlockSpec(memory_space=pltpu.VMEM)
    return pl.pallas_call(
        functools.partial(exchange_kernel, n_stream, n_span),
        out_shape=(
            jax.ShapeDtypeStruct((27, 8, 8, 128), F32),
            jax.ShapeDtypeStruct((4, 72, 128), F32),
            jax.ShapeDtypeStruct((4, 24, 128), F32),
            jax.ShapeDtypeStruct((5, 5, 32, 128), F32),
            jax.ShapeDtypeStruct((5, 5, 32, 128), F32),
            jax.ShapeDtypeStruct((4, 4, 27, 128), F32),
            jax.ShapeDtypeStruct((3, 32, 128), jnp.int32),
            jax.ShapeDtypeStruct((2, 2, 32, 128), F32),
            jax.ShapeDtypeStruct((9, 8, 128), jnp.int32),
        ),
        in_specs=[hbm] * 5,
        out_specs=(vmem,) * 9,
        scratch_shapes=[
            pltpu.VMEM((6, 6, 27, 128), F32),
            pltpu.VMEM((3, 3, 32, 64), F32),
            pltpu.VMEM((6, 6, 128), jnp.int32),
            pltpu.SMEM((16, 32), jnp.int32),
            pltpu.SMEM((27,), F32),
            pltpu.VMEM((8, 8, 128), jnp.int32),
            pltpu.VMEM((3, 8, 8, 128), jnp.int32),
            pltpu.VMEM((4, 72, 128), F32),
            pltpu.VMEM((4, 24, 128), F32),
            pltpu.SemaphoreType.DMA((5,)),
            pltpu.SemaphoreType.DMA((8,)),
            pltpu.SemaphoreType.DMA((8,)),
        ],
        compiler_params=pltpu.CompilerParams(
            collective_id=0, has_side_effects=True, vmem_limit_bytes=24 * 2**20
        ),
    )(*[pltpu.with_memory_space_constraint(arg, pltpu.HBM) for arg in args])


def forward(low, mid, high, speed, total=None):
    pair, diff = high + low, high - low
    if total is None:
        total = pair + 4.0 * mid
    first = diff - speed * total
    return total, first, pair - speed * (diff + first)


def backward(total, first, second, speed):
    slope = first + speed * total
    curve = second + speed * (first + slope)
    return curve - slope, 0.5 * (total - curve), curve + slope


def collide(g, keep, pull):
    t0 = [g[r] + g[18 + r] + 4.0 * g[9 + r] for r in range(9)]
    dx = [g[18 + r] - g[r] for r in range(9)]
    s0 = [t0[c] + t0[6 + c] + 4.0 * t0[3 + c] for c in range(3)]
    dy = [t0[6 + c] - t0[c] for c in range(3)]
    density = s0[0] + s0[2] + 4.0 * s0[1]
    ex = [dx[c] + dx[6 + c] + 4.0 * dx[3 + c] for c in range(3)]
    inverse = 1.0 / density
    ux = (ex[0] + ex[2] + 4.0 * ex[1]) * inverse
    uy = (dy[0] + dy[2] + 4.0 * dy[1]) * inverse
    uz = (s0[2] - s0[0]) * inverse
    k = [None] * 27
    for r in range(9):
        k[r], k[9 + r], k[18 + r] = forward(g[r], g[9 + r], g[18 + r], ux, t0[r])
    for a in range(3):
        for c in range(3):
            i = 9 * a + c
            k[i], k[i + 3], k[i + 6] = forward(k[i], k[i + 3], k[i + 6], uy, s0[c] if a == 0 else None)
    for i in range(0, 27, 3):
        k[i], k[i + 1], k[i + 2] = forward(k[i], k[i + 1], k[i + 2], uz, density if i == 0 else None)
    for q in range(27):
        k[q] = keep[q] * k[q] if 1 in (q // 9, q // 3 % 3, q % 3) else keep[q] * k[q] + pull[q] * density
    for i in range(0, 27, 3):
        k[i], k[i + 1], k[i + 2] = backward(k[i], k[i + 1], k[i + 2], uz)
    for a in range(3):
        for c in range(3):
            i = 9 * a + c
            k[i], k[i + 3], k[i + 6] = backward(k[i], k[i + 3], k[i + 6], uy)
    for r in range(9):
        k[r], k[9 + r], k[18 + r] = backward(k[r], k[9 + r], k[18 + r], ux)
    return k


def lane(shape):
    return lax.broadcasted_iota(jnp.int32, shape, len(shape) - 1)


def take(values, index):
    return jnp.take_along_axis(values, index, axis=1, mode="promise_in_bounds")


def stretch(values, half=0):
    at = lane(values.shape)
    middle = lax.shift_right_logical(at, 1)
    beside = jnp.clip(middle + 2 * (at & 1) - 1, 0, 63)
    return 0.75 * take(values, middle + 64 * half) + 0.25 * take(values, beside + 64 * half)


def shrink(values):
    at = lane(values.shape)
    even = jnp.minimum(2 * at, 126)
    return (take(values, even) + take(values, even + 1)) * 0.125


def mix(near, far):
    return 0.75 * near + 0.25 * far


def step_kernel(
    given, faces, corners, halo, tall, inner, coarse_stop, table, around, fine_next, coarse_next, turned,
    corner_raw, corner_tall, edge_x, edge_y, coarse_out, sems,
):
    inner_copy = pltpu.make_async_copy(inner, fine_next.at[pl.ds(1, 4), pl.ds(1, 4)], sems.at[0])
    inner_copy.start()
    x_copies = [pltpu.make_async_copy(edge_x.at[n], fine_next.at[5 * n], sems.at[1 + n]) for n in range(2)]
    y_copies = [
        pltpu.make_async_copy(edge_y.at[n], fine_next.at[pl.ds(1, 4), 5 * n], sems.at[3 + n]) for n in range(2)
    ]
    coarse_copy = pltpu.make_async_copy(coarse_out, coarse_next, sems.at[5])

    def level(n, rows):
        return around[n, pl.ds(0, rows), :] == 1

    def cell(x, y):
        if x % 5 == 0:
            return edge_x[x // 5, y]
        if y % 5 == 0:
            return edge_y[y // 5, x - 1]
        return inner[x - 1, y - 1]

    refined = jnp.max(around[0]) == 1
    for slot in range(4):
        unfold(corner_raw.at[slot], corner_tall.at[slot], corners[slot, pl.ds(0, 16), :])

    def tall_at(i, j, start, count):
        if i % 4 == 0 and j % 4 == 0:
            return corner_tall[i // 4 * 2 + j // 4, pl.ds(start, count), :]
        return tall[i, j, pl.ds(start, count), :]

    @pl.when(refined)
    def _():
        for slot, side in enumerate(FACES):
            dx, dy = side
            pops = face_pops(side)
            edge, inner = 2 + 2 * (dx + dy), 2 + (dx + dy)
            rim = 7 if dx + dy > 0 else 0
            first, count = (pops[0], 9) if dx else (0, 27)
            if dx:
                line = [mix(tall_at(edge, j, first, count), tall_at(inner, j, first, count)) for j in range(5)]
            else:
                line = [mix(tall_at(i, edge, first, count), tall_at(i, inner, first, count)) for i in range(5)]
            cells = []
            for n in range(6):
                cells.append(mix(line[n // 2 + 1], line[n // 2 + 2 * (n % 2)]))
            turn = jnp.swapaxes(jnp.stack(cells), 0, 1)
            fine_there = level(1 + slot, 6)
            for n, q in enumerate(pops):
                values = jnp.where(fine_there, faces[slot, pl.ds(6 * n, 6), :], turn[q - first])
                if dx:
                    turned[q, rim, pl.ds(1, 6), :] = values
                else:
                    turned[q, pl.ds(1, 6), rim, :] = values

        for slot, side in enumerate(CORNERS):
            dx, dy = side
            start = corner_start(side)
            ei, ii, ej, ij = 2 + 2 * dx, 2 + dx, 2 + 2 * dy, 2 + dy
            exploded = mix(
                mix(tall_at(ei, ej, start, 3), tall_at(ii, ej, start, 3)),
                mix(tall_at(ei, ij, start, 3), tall_at(ii, ij, start, 3)),
            )
            value = jnp.where(level(5 + slot, 3), corners[slot, pl.ds(16, 3), :], exploded)
            for c in range(3):
                turned[start + c, 7 if dx > 0 else 0, pl.ds(7 if dy > 0 else 0, 1), :] = value[c : c + 1]

        keep, pull = rates_of(table, 0)

        def advance(load, count):
            at = lane((count, 128))
            still = [load(q, 0, 0) for q in range(27)]
            g = []
            for q in range(27):
                ex, ey, ez = q // 9 - 1, q // 3 % 3 - 1, q % 3 - 1
                source = load(q, ex, ey) if ex or ey else still[q]
                if ez:
                    source = jnp.where(at == (0 if ez > 0 else 127), still[26 - q], pltpu.roll(source, ez % 128, 1))
                g.append(source)
            return jnp.swapaxes(jnp.stack(collide(g, keep, pull)), 0, 1)

        for n in range(2):
            edge_x[n] = advance(lambda q, ex, ey: turned[q, 5 * n + 1 - ex, pl.ds(1 - ey, 6), :], 6)
            x_copies[n].start()
        both = advance(
            lambda q, ex, ey: jnp.concatenate(
                [turned[q, pl.ds(2 - ex, 4), 1 - ey, :], turned[q, pl.ds(2 - ex, 4), 6 - ey, :]], axis=0
            ),
            8,
        )
        for n in range(2):
            edge_y[n] = both[4 * n : 4 * n + 4]
            y_copies[n].start()
        for i in range(3):
            for j in range(3):
                total = (cell(2 * i, 2 * j) + cell(2 * i, 2 * j + 1)) + (
                    cell(2 * i + 1, 2 * j) + cell(2 * i + 1, 2 * j + 1)
                )
                coarse_out[i, j] = shrink(total)[:, :64]
        coarse_copy.start()

    @pl.when(jnp.logical_not(refined))
    def _():
        for x in range(6):
            line = [mix(tall_at(x // 2 + 1, j, 0, 27), tall_at(x // 2 + 2 * (x % 2), j, 0, 27)) for j in range(5)]
            for y in range(6) if x % 5 == 0 else (0, 5):
                exploded = mix(line[y // 2 + 1], line[y // 2 + 2 * (y % 2)])
                if x % 5 == 0:
                    edge_x[x // 5, y] = exploded
                else:
                    edge_y[y // 5, x - 1] = exploded
            if x % 5 == 0:
                x_copies[x // 5].start()
        for n in range(2):
            y_copies[n].start()

        keep, pull = rates_of(table, 1)
        flat = turned.reshape(27 * 64, 128)
        for i in range(5):
            if i % 4 == 0:
                ends = [corner_raw[i // 4 * 2 + n, pl.ds(0, 27), :] for n in range(2)]
                cells = jnp.stack([ends[0]] + [halo[i, j, pl.ds(0, 27), :] for j in (1, 2, 3)] + [ends[1]])
            else:
                cells = halo[i, :, pl.ds(0, 27), :]
            cells = jnp.swapaxes(cells, 0, 1)
            for q in range(27):
                flat[pl.ds(64 * q + 5 * i, 5), :] = cells[q]
        g = []
        for q in range(27):
            ex, ey, ez = q // 9 - 1, q // 3 % 3 - 1, q % 3 - 1
            start = 6 - 5 * ex - ey
            source = flat[pl.ds(64 * q + start, 13), :]
            if ez:
                source = pltpu.roll(source, ez % 128, 1)
            if q != 13:
                stop = coarse_stop[ez + 1, pl.ds(start, 13), :]
                source = jnp.where(stop != 0, flat[pl.ds(64 * (26 - q) + 6, 13), :], source)
            g.append(source)
        new = collide(g, keep, pull)
        wall = coarse_stop[1, pl.ds(6, 13), :] != 0
        new = [jnp.where(wall, flat[pl.ds(64 * q + 6, 13), :], new[q]) for q in range(27)]
        turn = jnp.swapaxes(jnp.stack(new), 0, 1)
        for i in range(3):
            for j in range(3):
                coarse_out[i, j] = turn[5 * i + j][:, :64]
        coarse_copy.start()

    for copy in [inner_copy, coarse_copy] + x_copies + y_copies:
        copy.wait()


def step(*args):
    vmem = pl.BlockSpec(memory_space=pltpu.VMEM)
    hbm = pl.BlockSpec(memory_space=pltpu.HBM)
    return pl.pallas_call(
        step_kernel,
        out_shape=(
            jax.ShapeDtypeStruct((6, 6, 27, 128), F32),
            jax.ShapeDtypeStruct((3, 3, 27, 64), F32),
            jax.ShapeDtypeStruct((27, 8, 8, 128), F32),
        ),
        in_specs=[vmem] * 9,
        out_specs=(hbm, hbm, vmem),
        input_output_aliases={0: 2},
        scratch_shapes=[
            pltpu.VMEM((4, 32, 128), F32),
            pltpu.VMEM((4, 32, 128), F32),
            pltpu.VMEM((2, 6, 27, 128), F32),
            pltpu.VMEM((2, 4, 27, 128), F32),
            pltpu.VMEM((3, 3, 27, 64), F32),
            pltpu.SemaphoreType.DMA((6,)),
        ],
        compiler_params=pltpu.CompilerParams(vmem_limit_bytes=24 * 2**20),
    )(*args)


def solution(mesh):
    n_stream, n_span = mesh.shape["stream"], mesh.shape["span"]

    def local(fine_pops, coarse_pops, obstacle, block_level, relax_rates):
        fine = jnp.transpose(fine_pops, (1, 2, 0, 3))
        coarse = jnp.transpose(coarse_pops, (1, 2, 0, 3))
        ready = exchange(n_stream, n_span, fine, coarse, obstacle, block_level, relax_rates)
        fine_next, coarse_next, _ = step(*ready)
        return jnp.transpose(fine_next, (2, 0, 1, 3)), jnp.transpose(coarse_next, (2, 0, 1, 3))

    placed = P(None, "stream", "span", None)
    return jax.shard_map(
        local,
        mesh=mesh,
        in_specs=(placed, placed, P("stream", "span", None), P(), P()),
        out_specs=(placed, placed),
        check_vma=False,
    )
```

```python
import functools

import jax
import jax.numpy as jnp
from jax import lax
from jax.experimental import pallas as pl
from jax.experimental.pallas import tpu as pltpu
from jax.sharding import PartitionSpec as P

MESH = pl.DeviceIdType.MESH
F32 = jnp.float32
FACES = ((-1, 0), (1, 0), (0, -1), (0, 1))
CORNERS = ((-1, -1), (-1, 1), (1, -1), (1, 1))


def face_pops(side):
    dx, dy = side
    return [q for q in range(27) if (q // 9 - 1 == -dx if dx else q // 3 % 3 - 1 == -dy)]


def corner_start(side):
    dx, dy = side
    return 9 * (1 - dx) + 3 * (1 - dy)


def face_cells(side):
    dx, dy = side
    return [(1 - dx, j) for j in range(3)] if dx else [(i, 1 - dy) for i in range(3)]


def halo_cells(side):
    dx, dy = side
    return [(2 + 2 * dx, 1 + j) if dx else (1 + j, 2 + 2 * dy) for j in range(3)]


def end_pops(side):
    dx, dy = side
    return [face_pops((0, s) if dx else (s, 0)) for s in (-1, 1)]


def pick_rows(cell, pops):
    return jnp.concatenate([cell[q : q + 3] for q in pops[::3]], axis=0)


def rates_of(table, n):
    return [table[n, 0, pl.ds(q, 1), :] for q in range(27)], [table[n, 1, pl.ds(q, 1), :] for q in range(27)]


def unfold(raw, tall, fold):
    raw[pl.ds(0, 16), :] = fold
    raw[pl.ds(16, 16), :] = pltpu.roll(fold, 64, 1)
    tall[pl.ds(0, 16), :] = stretch(fold)
    tall[pl.ds(16, 16), :] = stretch(fold, 1)


def exchange_kernel(
    n_stream, n_span, fine, coarse, obstacle, level, rates,
    turned, faces, corners, ends_raw, tall, grid, inner, coarse_stop, table, around,
    halo, native, own, flags, levels, speeds, blocked, rolled, face_out, corner_out, load_sem, send_sem, recv_sem,
):
    row, col = lax.axis_index("stream"), lax.axis_index("span")

    def at(side):
        return (lax.rem(row + side[0] + n_stream, n_stream), lax.rem(col + side[1] + n_span, n_span))

    barrier = pltpu.get_barrier_semaphore()
    for side in CORNERS + FACES:
        pl.semaphore_signal(barrier, inc=1, device_id=at(side), device_id_type=MESH)
    for i in range(3):
        for j in range(3):
            own[i, j, pl.ds(24, 8), :] = jnp.zeros((8, 64), F32)
    loads = [
        pltpu.make_async_copy(fine, native, load_sem.at[0]),
        pltpu.make_async_copy(coarse, own.at[:, :, pl.ds(0, 27)], load_sem.at[1]),
        pltpu.make_async_copy(level, levels, load_sem.at[2]),
        pltpu.make_async_copy(obstacle, flags, load_sem.at[3]),
        pltpu.make_async_copy(rates, speeds, load_sem.at[4]),
    ]
    for load in loads:
        load.start()
    for load in loads[:3]:
        load.wait()
    here = levels[row, col]
    there = [levels[at(side)[0], at(side)[1]] for side in FACES + CORNERS]
    for slot, side in enumerate(CORNERS):
        dx, dy = side
        cell = own[1 - dx, 1 - dy]
        corner_out[slot, pl.ds(0, 16), :] = jnp.concatenate([cell[0:16], cell[16:32]], axis=1)
        corner_out[slot, pl.ds(16, 3), :] = native[
            5 if dx < 0 else 0, 5 if dy < 0 else 0, pl.ds(corner_start(side), 3), :
        ]
    for slot, side in enumerate(FACES):
        dx, dy = side
        both = (here == 1) & (there[FACES.index((-dx, -dy))] == 1)
        cells = [own[i, j] for i, j in face_cells(side)]
        face_out[slot, pl.ds(0, 32), :] = jnp.concatenate([cells[0], cells[1]], axis=1)
        face_out[slot, pl.ds(32, 16), :] = jnp.concatenate([cells[2][0:16], cells[2][16:32]], axis=1)
        face_out[slot, pl.ds(48, 8), :] = jnp.zeros((8, 128), F32)
        edge = native[5 if dx < 0 else 0] if dx else native[:, 5 if dy < 0 else 0]
        edge = jnp.swapaxes(edge, 0, 1)
        for n, q in enumerate(face_pops(side)):
            spot = face_out.at[slot, pl.ds(6 * n, 6)]
            spot[...] = jnp.where(both, edge[q], spot[...])
        ends = [pick_rows(cell, pops) for cell, pops in zip((cells[0], cells[2]), end_pops(side))]
        face_out[slot, pl.ds(56, 9), :] = jnp.concatenate(ends, axis=1)
    pl.semaphore_wait(barrier, 8)
    copies = []
    for slot, (dx, dy) in enumerate(CORNERS):
        copies.append(
            pltpu.make_async_remote_copy(
                corner_out.at[slot, pl.ds(0, 19)], corners.at[slot, pl.ds(0, 19)],
                send_sem.at[4 + slot], recv_sem.at[4 + slot], device_id=at((-dx, -dy)), device_id_type=MESH,
            )
        )
    for slot, (dx, dy) in enumerate(FACES):
        copies.append(
            pltpu.make_async_remote_copy(
                face_out.at[slot, pl.ds(0, 65)], faces.at[slot, pl.ds(0, 65)],
                send_sem.at[slot], recv_sem.at[slot], device_id=at((-dx, -dy)), device_id_type=MESH,
            )
        )
    for copy in copies:
        copy.start()
    for x in range(6):
        turned[:, x + 1, pl.ds(1, 6), :] = jnp.swapaxes(native[x], 0, 1)
    for i in range(3):
        for j in range(3):
            cell = own[i, j]
            halo[i + 1, j + 1, :, pl.ds(0, 64)] = cell
            tall[i + 1, j + 1] = stretch(jnp.concatenate([cell, cell], axis=1))
    for n, value in enumerate([here] + there):
        around[n] = jnp.full((8, 128), value, jnp.int32)
    for load in loads[3:]:
        load.wait()
    for q in range(27):
        orders = (q // 9, q // 3 % 3, q % 3)
        share = 0.0 if 1 in orders else 0.125 / 3.0 ** orders.count(2)
        fine_rate = jnp.full((1, 128), speeds[q], F32)
        for n, rate in enumerate((fine_rate, 1.0 / (2.0 / fine_rate - 0.5))):
            table[n, 0, pl.ds(q, 1), :] = (1.0 - rate) * 0.125
            table[n, 1, pl.ds(q, 1), :] = rate * share
    blocked[...] = jnp.zeros_like(blocked)
    blocked[pl.ds(1, 6), pl.ds(1, 6), :] = flags[...]
    rows = lane((8, 128))
    for x in range(8):
        stop = blocked[x]
        rolled[1, x] = stop
        rolled[2, x] = jnp.where(rows == 0, 1, pltpu.roll(stop, 1, 1))
        rolled[0, x] = jnp.where(rows == 127, 1, pltpu.roll(stop, 127, 1))
    stop = jnp.maximum(jnp.maximum(blocked[3], blocked[4]), pltpu.roll(jnp.maximum(blocked[3], blocked[4]), 7, 0))
    even = jnp.minimum(2 * rows, 126)
    stop = jnp.where(rows < 64, jnp.maximum(take(stop, even), take(stop, even + 1)), 0)
    coarse_stop[...] = jnp.zeros_like(coarse_stop)
    coarse_stop[1, pl.ds(12, 1), :] = stop[3:4]
    high = lane((32, 128))
    coarse_stop[2] = jnp.where(high == 0, 1, pltpu.roll(coarse_stop[1], 1, 1))
    coarse_stop[0] = jnp.where(high == 63, 1, pltpu.roll(coarse_stop[1], 127, 1))

    def middle(x, carry):
        keep, pull = rates_of(table, 0)
        g = []
        for q in range(27):
            ex, ey, ez = q // 9 - 1, q // 3 % 3 - 1, q % 3 - 1
            source = turned[q, x + 1 - ex, pl.ds(1 - ey, 6), :]
            if ez:
                source = pltpu.roll(source, ez % 128, 1)
            if q != 13:
                stop = rolled[ez + 1, x + 1 - ex, pl.ds(1 - ey, 6), :]
                source = jnp.where(stop != 0, turned[26 - q, x + 1, pl.ds(1, 6), :], source)
            g.append(source)
        new = collide(g, keep, pull)
        wall = blocked[x + 1, pl.ds(1, 6), :] != 0
        new = [jnp.where(wall, turned[q, x + 1, pl.ds(1, 6), :], new[q]) for q in range(27)]
        inner[x - 1] = jnp.swapaxes(jnp.stack(new), 0, 1)[1:5]
        return carry

    lax.fori_loop(1, 5, middle, 0)
    for x in range(1, 5):
        line = [mix(tall[x // 2 + 1, j, pl.ds(0, 27), :], tall[x // 2 + 2 * (x % 2), j, pl.ds(0, 27), :]) for j in (1, 2, 3)]
        for y in range(1, 5):
            exploded = mix(line[y // 2], line[y // 2 - 1 + 2 * (y % 2)])
            inner[x - 1, y - 1] = jnp.where(here == 1, inner[x - 1, y - 1], exploded)
    for slot, side in enumerate(FACES):
        copies[4 + slot].wait()
        pair, fold = faces[slot, pl.ds(0, 32), :], faces[slot, pl.ds(32, 16), :]
        spots = halo_cells(side)
        halo[spots[0][0], spots[0][1]] = pair
        halo[spots[1][0], spots[1][1]] = pltpu.roll(pair, 64, 1)
        tall[spots[0][0], spots[0][1]] = stretch(pair)
        tall[spots[1][0], spots[1][1]] = stretch(pair, 1)
        unfold(halo.at[spots[2][0], spots[2][1]], tall.at[spots[2][0], spots[2][1]], fold)
        both = (here == 1) & (there[slot] == 1)
        ends = faces[slot, pl.ds(56, 9), :]
        for half, (spot, pops) in enumerate(zip((spots[0], spots[2]), end_pops(side))):
            rows = stretch(ends, half)
            for n in (0, 3, 6):
                place = tall.at[spot[0], spot[1], pl.ds(pops[n], 3)]
                place[...] = jnp.where(both, rows[n : n + 3], place[...])
    for i in (1, 2, 3):
        cells = jnp.swapaxes(halo[i, :, pl.ds(0, 27), :], 0, 1)
        for q in range(27):
            grid[q, pl.ds(5 * i, 5), :] = cells[q]
    for n, i in enumerate((0, 4)):
        for j in (1, 2, 3):
            ends_raw[n, j] = halo[i, j]
    for copy in copies[:4]:
        copy.wait()


def exchange(n_stream, n_span, *args):
    hbm = pl.BlockSpec(memory_space=pltpu.HBM)
    vmem = pl.BlockSpec(memory_space=pltpu.VMEM)
    return pl.pallas_call(
        functools.partial(exchange_kernel, n_stream, n_span),
        out_shape=(
            jax.ShapeDtypeStruct((27, 8, 8, 128), F32),
            jax.ShapeDtypeStruct((4, 72, 128), F32),
            jax.ShapeDtypeStruct((4, 24, 128), F32),
            jax.ShapeDtypeStruct((2, 5, 32, 128), F32),
            jax.ShapeDtypeStruct((5, 5, 32, 128), F32),
            jax.ShapeDtypeStruct((27, 32, 128), F32),
            jax.ShapeDtypeStruct((4, 4, 27, 128), F32),
            jax.ShapeDtypeStruct((3, 32, 128), jnp.int32),
            jax.ShapeDtypeStruct((2, 2, 32, 128), F32),
            jax.ShapeDtypeStruct((9, 8, 128), jnp.int32),
        ),
        in_specs=[hbm] * 5,
        out_specs=(vmem,) * 10,
        scratch_shapes=[
            pltpu.VMEM((5, 5, 32, 128), F32),
            pltpu.VMEM((6, 6, 27, 128), F32),
            pltpu.VMEM((3, 3, 32, 64), F32),
            pltpu.VMEM((6, 6, 128), jnp.int32),
            pltpu.SMEM((16, 32), jnp.int32),
            pltpu.SMEM((27,), F32),
            pltpu.VMEM((8, 8, 128), jnp.int32),
            pltpu.VMEM((3, 8, 8, 128), jnp.int32),
            pltpu.VMEM((4, 72, 128), F32),
            pltpu.VMEM((4, 24, 128), F32),
            pltpu.SemaphoreType.DMA((5,)),
            pltpu.SemaphoreType.DMA((8,)),
            pltpu.SemaphoreType.DMA((8,)),
        ],
        compiler_params=pltpu.CompilerParams(
            collective_id=0, has_side_effects=True, vmem_limit_bytes=24 * 2**20
        ),
    )(*[pltpu.with_memory_space_constraint(arg, pltpu.HBM) for arg in args])


def forward(low, mid, high, speed, total=None):
    pair, diff = high + low, high - low
    if total is None:
        total = pair + 4.0 * mid
    first = diff - speed * total
    return total, first, pair - speed * (diff + first)


def backward(total, first, second, speed):
    slope = first + speed * total
    curve = second + speed * (first + slope)
    return curve - slope, 0.5 * (total - curve), curve + slope


def collide(g, keep, pull):
    t0 = [g[r] + g[18 + r] + 4.0 * g[9 + r] for r in range(9)]
    dx = [g[18 + r] - g[r] for r in range(9)]
    s0 = [t0[c] + t0[6 + c] + 4.0 * t0[3 + c] for c in range(3)]
    dy = [t0[6 + c] - t0[c] for c in range(3)]
    density = s0[0] + s0[2] + 4.0 * s0[1]
    ex = [dx[c] + dx[6 + c] + 4.0 * dx[3 + c] for c in range(3)]
    inverse = 1.0 / density
    ux = (ex[0] + ex[2] + 4.0 * ex[1]) * inverse
    uy = (dy[0] + dy[2] + 4.0 * dy[1]) * inverse
    uz = (s0[2] - s0[0]) * inverse
    k = [None] * 27
    for r in range(9):
        k[r], k[9 + r], k[18 + r] = forward(g[r], g[9 + r], g[18 + r], ux, t0[r])
    for a in range(3):
        for c in range(3):
            i = 9 * a + c
            k[i], k[i + 3], k[i + 6] = forward(k[i], k[i + 3], k[i + 6], uy, s0[c] if a == 0 else None)
    for i in range(0, 27, 3):
        k[i], k[i + 1], k[i + 2] = forward(k[i], k[i + 1], k[i + 2], uz, density if i == 0 else None)
    for q in range(27):
        k[q] = keep[q] * k[q] if 1 in (q // 9, q // 3 % 3, q % 3) else keep[q] * k[q] + pull[q] * density
    for i in range(0, 27, 3):
        k[i], k[i + 1], k[i + 2] = backward(k[i], k[i + 1], k[i + 2], uz)
    for a in range(3):
        for c in range(3):
            i = 9 * a + c
            k[i], k[i + 3], k[i + 6] = backward(k[i], k[i + 3], k[i + 6], uy)
    for r in range(9):
        k[r], k[9 + r], k[18 + r] = backward(k[r], k[9 + r], k[18 + r], ux)
    return k


def lane(shape):
    return lax.broadcasted_iota(jnp.int32, shape, len(shape) - 1)


def take(values, index):
    return jnp.take_along_axis(values, index, axis=1, mode="promise_in_bounds")


def stretch(values, half=0):
    at = lane(values.shape)
    middle = lax.shift_right_logical(at, 1)
    beside = jnp.clip(middle + 2 * (at & 1) - 1, 0, 63)
    return 0.75 * take(values, middle + 64 * half) + 0.25 * take(values, beside + 64 * half)


def shrink(values):
    at = lane(values.shape)
    even = jnp.minimum(2 * at, 126)
    return (take(values, even) + take(values, even + 1)) * 0.125


def mix(near, far):
    return 0.75 * near + 0.25 * far


def step_kernel(
    given, faces, corners, ends_raw, tall, middle, inner, coarse_stop, table, around,
    fine_next, coarse_next, turned, grid,
    corner_raw, corner_tall, edge_x, edge_y, coarse_out, sems,
):
    inner_copy = pltpu.make_async_copy(inner, fine_next.at[pl.ds(1, 4), pl.ds(1, 4)], sems.at[0])
    inner_copy.start()
    x_copies = [pltpu.make_async_copy(edge_x.at[n], fine_next.at[5 * n], sems.at[1 + n]) for n in range(2)]
    y_copies = [
        pltpu.make_async_copy(edge_y.at[n], fine_next.at[pl.ds(1, 4), 5 * n], sems.at[3 + n]) for n in range(2)
    ]
    coarse_copy = pltpu.make_async_copy(coarse_out, coarse_next, sems.at[5])

    def level(n, rows):
        return around[n, pl.ds(0, rows), :] == 1

    def cell(x, y):
        if x % 5 == 0:
            return edge_x[x // 5, y]
        if y % 5 == 0:
            return edge_y[y // 5, x - 1]
        return inner[x - 1, y - 1]

    refined = jnp.max(around[0]) == 1
    for slot in range(4):
        unfold(corner_raw.at[slot], corner_tall.at[slot], corners[slot, pl.ds(0, 16), :])

    def tall_at(i, j, start, count):
        if i % 4 == 0 and j % 4 == 0:
            return corner_tall[i // 4 * 2 + j // 4, pl.ds(start, count), :]
        return tall[i, j, pl.ds(start, count), :]

    @pl.when(refined)
    def _():
        for slot, side in enumerate(FACES):
            dx, dy = side
            pops = face_pops(side)
            edge, inner = 2 + 2 * (dx + dy), 2 + (dx + dy)
            rim = 7 if dx + dy > 0 else 0
            first, count = (pops[0], 9) if dx else (0, 27)
            if dx:
                line = [mix(tall_at(edge, j, first, count), tall_at(inner, j, first, count)) for j in range(5)]
            else:
                line = [mix(tall_at(i, edge, first, count), tall_at(i, inner, first, count)) for i in range(5)]
            cells = []
            for n in range(6):
                cells.append(mix(line[n // 2 + 1], line[n // 2 + 2 * (n % 2)]))
            turn = jnp.swapaxes(jnp.stack(cells), 0, 1)
            fine_there = level(1 + slot, 6)
            for n, q in enumerate(pops):
                values = jnp.where(fine_there, faces[slot, pl.ds(6 * n, 6), :], turn[q - first])
                if dx:
                    turned[q, rim, pl.ds(1, 6), :] = values
                else:
                    turned[q, pl.ds(1, 6), rim, :] = values

        for slot, side in enumerate(CORNERS):
            dx, dy = side
            start = corner_start(side)
            ei, ii, ej, ij = 2 + 2 * dx, 2 + dx, 2 + 2 * dy, 2 + dy
            exploded = mix(
                mix(tall_at(ei, ej, start, 3), tall_at(ii, ej, start, 3)),
                mix(tall_at(ei, ij, start, 3), tall_at(ii, ij, start, 3)),
            )
            value = jnp.where(level(5 + slot, 3), corners[slot, pl.ds(16, 3), :], exploded)
            for c in range(3):
                turned[start + c, 7 if dx > 0 else 0, pl.ds(7 if dy > 0 else 0, 1), :] = value[c : c + 1]

        keep, pull = rates_of(table, 0)

        def advance(load, count):
            at = lane((count, 128))
            still = [load(q, 0, 0) for q in range(27)]
            g = []
            for q in range(27):
                ex, ey, ez = q // 9 - 1, q // 3 % 3 - 1, q % 3 - 1
                source = load(q, ex, ey) if ex or ey else still[q]
                if ez:
                    source = jnp.where(at == (0 if ez > 0 else 127), still[26 - q], pltpu.roll(source, ez % 128, 1))
                g.append(source)
            return jnp.swapaxes(jnp.stack(collide(g, keep, pull)), 0, 1)

        for n in range(2):
            edge_x[n] = advance(lambda q, ex, ey: turned[q, 5 * n + 1 - ex, pl.ds(1 - ey, 6), :], 6)
            x_copies[n].start()
        both = advance(
            lambda q, ex, ey: jnp.concatenate(
                [turned[q, pl.ds(2 - ex, 4), 1 - ey, :], turned[q, pl.ds(2 - ex, 4), 6 - ey, :]], axis=0
            ),
            8,
        )
        for n in range(2):
            edge_y[n] = both[4 * n : 4 * n + 4]
            y_copies[n].start()
        for i in range(3):
            for j in range(3):
                total = (cell(2 * i, 2 * j) + cell(2 * i, 2 * j + 1)) + (
                    cell(2 * i + 1, 2 * j) + cell(2 * i + 1, 2 * j + 1)
                )
                coarse_out[i, j] = shrink(total)[:, :64]
        coarse_copy.start()

    @pl.when(jnp.logical_not(refined))
    def _():
        for x in range(6):
            line = [mix(tall_at(x // 2 + 1, j, 0, 27), tall_at(x // 2 + 2 * (x % 2), j, 0, 27)) for j in range(5)]
            for y in range(6) if x % 5 == 0 else (0, 5):
                exploded = mix(line[y // 2 + 1], line[y // 2 + 2 * (y % 2)])
                if x % 5 == 0:
                    edge_x[x // 5, y] = exploded
                else:
                    edge_y[y // 5, x - 1] = exploded
            if x % 5 == 0:
                x_copies[x // 5].start()
        for n in range(2):
            y_copies[n].start()

        keep, pull = rates_of(table, 1)
        for n in range(2):
            cells = [ends_raw[n, j, pl.ds(0, 27), :] for j in (1, 2, 3)]
            cells = [corner_raw[2 * n, pl.ds(0, 27), :]] + cells + [corner_raw[2 * n + 1, pl.ds(0, 27), :]]
            cells = jnp.swapaxes(jnp.stack(cells), 0, 1)
            for q in range(27):
                grid[q, pl.ds(20 * n, 5), :] = cells[q]
        g = []
        for q in range(27):
            ex, ey, ez = q // 9 - 1, q // 3 % 3 - 1, q % 3 - 1
            start = 6 - 5 * ex - ey
            source = grid[q, pl.ds(start, 13), :]
            if ez:
                source = pltpu.roll(source, ez % 128, 1)
            if q != 13:
                stop = coarse_stop[ez + 1, pl.ds(start, 13), :]
                source = jnp.where(stop != 0, grid[26 - q, pl.ds(6, 13), :], source)
            g.append(source)
        new = collide(g, keep, pull)
        wall = coarse_stop[1, pl.ds(6, 13), :] != 0
        new = [jnp.where(wall, grid[q, pl.ds(6, 13), :], new[q]) for q in range(27)]
        turn = jnp.swapaxes(jnp.stack(new), 0, 1)
        for i in range(3):
            for j in range(3):
                coarse_out[i, j] = turn[5 * i + j][:, :64]
        coarse_copy.start()

    for copy in [inner_copy, coarse_copy] + x_copies + y_copies:
        copy.wait()


def step(*args):
    vmem = pl.BlockSpec(memory_space=pltpu.VMEM)
    hbm = pl.BlockSpec(memory_space=pltpu.HBM)
    return pl.pallas_call(
        step_kernel,
        out_shape=(
            jax.ShapeDtypeStruct((6, 6, 27, 128), F32),
            jax.ShapeDtypeStruct((3, 3, 27, 64), F32),
            jax.ShapeDtypeStruct((27, 8, 8, 128), F32),
            jax.ShapeDtypeStruct((27, 32, 128), F32),
        ),
        in_specs=[vmem] * 10,
        out_specs=(hbm, hbm, vmem, vmem),
        input_output_aliases={0: 2, 5: 3},
        scratch_shapes=[
            pltpu.VMEM((4, 32, 128), F32),
            pltpu.VMEM((4, 32, 128), F32),
            pltpu.VMEM((2, 6, 27, 128), F32),
            pltpu.VMEM((2, 4, 27, 128), F32),
            pltpu.VMEM((3, 3, 27, 64), F32),
            pltpu.SemaphoreType.DMA((6,)),
        ],
        compiler_params=pltpu.CompilerParams(vmem_limit_bytes=24 * 2**20),
    )(*args)


def solution(mesh):
    n_stream, n_span = mesh.shape["stream"], mesh.shape["span"]

    def local(fine_pops, coarse_pops, obstacle, block_level, relax_rates):
        fine = jnp.transpose(fine_pops, (1, 2, 0, 3))
        coarse = jnp.transpose(coarse_pops, (1, 2, 0, 3))
        ready = exchange(n_stream, n_span, fine, coarse, obstacle, block_level, relax_rates)
        fine_next, coarse_next, *_ = step(*ready)
        return jnp.transpose(fine_next, (2, 0, 1, 3)), jnp.transpose(coarse_next, (2, 0, 1, 3))

    placed = P(None, "stream", "span", None)
    return jax.shard_map(
        local,
        mesh=mesh,
        in_specs=(placed, placed, P("stream", "span", None), P(), P()),
        out_specs=(placed, placed),
        check_vma=False,
    )
```

```python
import functools

import jax
import jax.numpy as jnp
from jax import lax
from jax.experimental import pallas as pl
from jax.experimental.pallas import tpu as pltpu
from jax.sharding import PartitionSpec as P

MESH = pl.DeviceIdType.MESH
F32 = jnp.float32
FACES = ((-1, 0), (1, 0), (0, -1), (0, 1))
CORNERS = ((-1, -1), (-1, 1), (1, -1), (1, 1))


def face_pops(side):
    dx, dy = side
    return [q for q in range(27) if (q // 9 - 1 == -dx if dx else q // 3 % 3 - 1 == -dy)]


def corner_start(side):
    dx, dy = side
    return 9 * (1 - dx) + 3 * (1 - dy)


def face_cells(side):
    dx, dy = side
    return [(1 - dx, j) for j in range(3)] if dx else [(i, 1 - dy) for i in range(3)]


def halo_cells(side):
    dx, dy = side
    return [(2 + 2 * dx, 1 + j) if dx else (1 + j, 2 + 2 * dy) for j in range(3)]


def end_pops(side):
    dx, dy = side
    return [face_pops((0, s) if dx else (s, 0)) for s in (-1, 1)]


def pick_rows(cell, pops):
    return jnp.concatenate([cell[q : q + 3] for q in pops[::3]], axis=0)


def rates_of(table, n):
    return [table[n, 0, pl.ds(q, 1), :] for q in range(27)], [table[n, 1, pl.ds(q, 1), :] for q in range(27)]


def unfold(raw, tall, fold):
    raw[pl.ds(0, 16), :] = fold
    raw[pl.ds(16, 16), :] = pltpu.roll(fold, 64, 1)
    tall[pl.ds(0, 16), :] = stretch(fold)
    tall[pl.ds(16, 16), :] = stretch(fold, 1)


def exchange_kernel(
    n_stream, n_span, fine, coarse, obstacle, level, rates,
    turned, faces, corners, ends_raw, tall, grid, inner, sums, coarse_stop, table, around,
    halo, native, own, flags, levels, speeds, blocked, rolled, face_out, corner_out, load_sem, send_sem, recv_sem,
):
    row, col = lax.axis_index("stream"), lax.axis_index("span")

    def at(side):
        return (lax.rem(row + side[0] + n_stream, n_stream), lax.rem(col + side[1] + n_span, n_span))

    barrier = pltpu.get_barrier_semaphore()
    for side in CORNERS + FACES:
        pl.semaphore_signal(barrier, inc=1, device_id=at(side), device_id_type=MESH)
    for i in range(3):
        for j in range(3):
            own[i, j, pl.ds(24, 8), :] = jnp.zeros((8, 64), F32)
    loads = [
        pltpu.make_async_copy(fine, native, load_sem.at[0]),
        pltpu.make_async_copy(coarse, own.at[:, :, pl.ds(0, 27)], load_sem.at[1]),
        pltpu.make_async_copy(level, levels, load_sem.at[2]),
        pltpu.make_async_copy(obstacle, flags, load_sem.at[3]),
        pltpu.make_async_copy(rates, speeds, load_sem.at[4]),
    ]
    for load in loads:
        load.start()
    for load in loads[:3]:
        load.wait()
    here = levels[row, col]
    there = [levels[at(side)[0], at(side)[1]] for side in FACES + CORNERS]
    for slot, side in enumerate(CORNERS):
        dx, dy = side
        cell = own[1 - dx, 1 - dy]
        corner_out[slot, pl.ds(0, 16), :] = jnp.concatenate([cell[0:16], cell[16:32]], axis=1)
        corner_out[slot, pl.ds(16, 3), :] = native[
            5 if dx < 0 else 0, 5 if dy < 0 else 0, pl.ds(corner_start(side), 3), :
        ]
    for slot, side in enumerate(FACES):
        dx, dy = side
        both = (here == 1) & (there[FACES.index((-dx, -dy))] == 1)
        cells = [own[i, j] for i, j in face_cells(side)]
        face_out[slot, pl.ds(0, 32), :] = jnp.concatenate([cells[0], cells[1]], axis=1)
        face_out[slot, pl.ds(32, 16), :] = jnp.concatenate([cells[2][0:16], cells[2][16:32]], axis=1)
        face_out[slot, pl.ds(48, 8), :] = jnp.zeros((8, 128), F32)
        edge = native[5 if dx < 0 else 0] if dx else native[:, 5 if dy < 0 else 0]
        edge = jnp.swapaxes(edge, 0, 1)
        for n, q in enumerate(face_pops(side)):
            spot = face_out.at[slot, pl.ds(6 * n, 6)]
            spot[...] = jnp.where(both, edge[q], spot[...])
        ends = [pick_rows(cell, pops) for cell, pops in zip((cells[0], cells[2]), end_pops(side))]
        face_out[slot, pl.ds(56, 9), :] = jnp.concatenate(ends, axis=1)
    pl.semaphore_wait(barrier, 8)
    copies = []
    for slot, (dx, dy) in enumerate(CORNERS):
        copies.append(
            pltpu.make_async_remote_copy(
                corner_out.at[slot, pl.ds(0, 19)], corners.at[slot, pl.ds(0, 19)],
                send_sem.at[4 + slot], recv_sem.at[4 + slot], device_id=at((-dx, -dy)), device_id_type=MESH,
            )
        )
    for slot, (dx, dy) in enumerate(FACES):
        copies.append(
            pltpu.make_async_remote_copy(
                face_out.at[slot, pl.ds(0, 65)], faces.at[slot, pl.ds(0, 65)],
                send_sem.at[slot], recv_sem.at[slot], device_id=at((-dx, -dy)), device_id_type=MESH,
            )
        )
    for copy in copies:
        copy.start()
    for x in range(6):
        turned[:, x + 1, pl.ds(1, 6), :] = jnp.swapaxes(native[x], 0, 1)
    for i in range(3):
        for j in range(3):
            cell = own[i, j]
            halo[i + 1, j + 1, :, pl.ds(0, 64)] = cell
            tall[i + 1, j + 1] = stretch(jnp.concatenate([cell, cell], axis=1))
    for n, value in enumerate([here] + there):
        around[n] = jnp.full((8, 128), value, jnp.int32)
    for load in loads[3:]:
        load.wait()
    for q in range(27):
        orders = (q // 9, q // 3 % 3, q % 3)
        share = 0.0 if 1 in orders else 0.125 / 3.0 ** orders.count(2)
        fine_rate = jnp.full((1, 128), speeds[q], F32)
        for n, rate in enumerate((fine_rate, 1.0 / (2.0 / fine_rate - 0.5))):
            table[n, 0, pl.ds(q, 1), :] = (1.0 - rate) * 0.125
            table[n, 1, pl.ds(q, 1), :] = rate * share
    blocked[...] = jnp.zeros_like(blocked)
    blocked[pl.ds(1, 6), pl.ds(1, 6), :] = flags[...]
    rows = lane((8, 128))
    for x in range(8):
        stop = blocked[x]
        rolled[1, x] = stop
        rolled[2, x] = jnp.where(rows == 0, 1, pltpu.roll(stop, 1, 1))
        rolled[0, x] = jnp.where(rows == 127, 1, pltpu.roll(stop, 127, 1))
    stop = jnp.maximum(jnp.maximum(blocked[3], blocked[4]), pltpu.roll(jnp.maximum(blocked[3], blocked[4]), 7, 0))
    even = jnp.minimum(2 * rows, 126)
    stop = jnp.where(rows < 64, jnp.maximum(take(stop, even), take(stop, even + 1)), 0)
    coarse_stop[...] = jnp.zeros_like(coarse_stop)
    coarse_stop[1, pl.ds(12, 1), :] = stop[3:4]
    high = lane((32, 128))
    coarse_stop[2] = jnp.where(high == 0, 1, pltpu.roll(coarse_stop[1], 1, 1))
    coarse_stop[0] = jnp.where(high == 63, 1, pltpu.roll(coarse_stop[1], 127, 1))

    def middle(x, carry):
        keep, pull = rates_of(table, 0)
        g = []
        for q in range(27):
            ex, ey, ez = q // 9 - 1, q // 3 % 3 - 1, q % 3 - 1
            source = turned[q, x + 1 - ex, pl.ds(1 - ey, 6), :]
            if ez:
                source = pltpu.roll(source, ez % 128, 1)
            if q != 13:
                stop = rolled[ez + 1, x + 1 - ex, pl.ds(1 - ey, 6), :]
                source = jnp.where(stop != 0, turned[26 - q, x + 1, pl.ds(1, 6), :], source)
            g.append(source)
        new = collide(g, keep, pull)
        wall = blocked[x + 1, pl.ds(1, 6), :] != 0
        new = [jnp.where(wall, turned[q, x + 1, pl.ds(1, 6), :], new[q]) for q in range(27)]
        inner[x - 1] = jnp.swapaxes(jnp.stack(new), 0, 1)[1:5]
        return carry

    lax.fori_loop(1, 5, middle, 0)
    for x in range(1, 5):
        line = [mix(tall[x // 2 + 1, j, pl.ds(0, 27), :], tall[x // 2 + 2 * (x % 2), j, pl.ds(0, 27), :]) for j in (1, 2, 3)]
        for y in range(1, 5):
            exploded = mix(line[y // 2], line[y // 2 - 1 + 2 * (y % 2)])
            inner[x - 1, y - 1] = jnp.where(here == 1, inner[x - 1, y - 1], exploded)
    for i in range(3):
        for j in range(3):
            xs = [x for x in (2 * i, 2 * i + 1) if x % 5]
            parts = [inner[x - 1, y - 1] for x in xs for y in (2 * j, 2 * j + 1) if y % 5]
            sums[i, j] = functools.reduce(jnp.add, parts)
    for slot, side in enumerate(FACES):
        copies[4 + slot].wait()
        pair, fold = faces[slot, pl.ds(0, 32), :], faces[slot, pl.ds(32, 16), :]
        spots = halo_cells(side)
        raw = [ends_raw.at[i // 4, j] if i % 4 == 0 else halo.at[i, j] for i, j in spots]
        raw[0][...] = pair
        raw[1][...] = pltpu.roll(pair, 64, 1)
        tall[spots[0][0], spots[0][1]] = stretch(pair)
        tall[spots[1][0], spots[1][1]] = stretch(pair, 1)
        unfold(raw[2], tall.at[spots[2][0], spots[2][1]], fold)
        ends = faces[slot, pl.ds(56, 9), :]
        for half, (spot, pops) in enumerate(zip((spots[0], spots[2]), end_pops(side))):
            rows = stretch(ends, half)
            for n in (0, 3, 6):
                tall[spot[0], spot[1], pl.ds(pops[n], 3), :] = rows[n : n + 3]
    for i in (1, 2, 3):
        cells = jnp.swapaxes(halo[i, :, pl.ds(0, 27), :], 0, 1)
        for q in range(27):
            grid[q, pl.ds(5 * i, 5), :] = cells[q]
    for copy in copies[:4]:
        copy.wait()


def exchange(n_stream, n_span, *args):
    hbm = pl.BlockSpec(memory_space=pltpu.HBM)
    vmem = pl.BlockSpec(memory_space=pltpu.VMEM)
    return pl.pallas_call(
        functools.partial(exchange_kernel, n_stream, n_span),
        out_shape=(
            jax.ShapeDtypeStruct((27, 8, 8, 128), F32),
            jax.ShapeDtypeStruct((4, 72, 128), F32),
            jax.ShapeDtypeStruct((4, 24, 128), F32),
            jax.ShapeDtypeStruct((2, 5, 32, 128), F32),
            jax.ShapeDtypeStruct((5, 5, 32, 128), F32),
            jax.ShapeDtypeStruct((27, 32, 128), F32),
            jax.ShapeDtypeStruct((4, 4, 27, 128), F32),
            jax.ShapeDtypeStruct((3, 3, 27, 128), F32),
            jax.ShapeDtypeStruct((3, 32, 128), jnp.int32),
            jax.ShapeDtypeStruct((2, 2, 32, 128), F32),
            jax.ShapeDtypeStruct((9, 8, 128), jnp.int32),
        ),
        in_specs=[hbm] * 5,
        out_specs=(vmem,) * 11,
        scratch_shapes=[
            pltpu.VMEM((5, 5, 32, 128), F32),
            pltpu.VMEM((6, 6, 27, 128), F32),
            pltpu.VMEM((3, 3, 32, 64), F32),
            pltpu.VMEM((6, 6, 128), jnp.int32),
            pltpu.SMEM((16, 32), jnp.int32),
            pltpu.SMEM((27,), F32),
            pltpu.VMEM((8, 8, 128), jnp.int32),
            pltpu.VMEM((3, 8, 8, 128), jnp.int32),
            pltpu.VMEM((4, 72, 128), F32),
            pltpu.VMEM((4, 24, 128), F32),
            pltpu.SemaphoreType.DMA((5,)),
            pltpu.SemaphoreType.DMA((8,)),
            pltpu.SemaphoreType.DMA((8,)),
        ],
        compiler_params=pltpu.CompilerParams(
            collective_id=0, has_side_effects=True, vmem_limit_bytes=24 * 2**20
        ),
    )(*[pltpu.with_memory_space_constraint(arg, pltpu.HBM) for arg in args])


def forward(low, mid, high, speed, total=None):
    pair, diff = high + low, high - low
    if total is None:
        total = pair + 4.0 * mid
    first = diff - speed * total
    return total, first, pair - speed * (diff + first)


def backward(total, first, second, speed):
    slope = first + speed * total
    curve = second + speed * (first + slope)
    return curve - slope, 0.5 * (total - curve), curve + slope


def collide(g, keep, pull):
    t0 = [g[r] + g[18 + r] + 4.0 * g[9 + r] for r in range(9)]
    dx = [g[18 + r] - g[r] for r in range(9)]
    s0 = [t0[c] + t0[6 + c] + 4.0 * t0[3 + c] for c in range(3)]
    dy = [t0[6 + c] - t0[c] for c in range(3)]
    density = s0[0] + s0[2] + 4.0 * s0[1]
    ex = [dx[c] + dx[6 + c] + 4.0 * dx[3 + c] for c in range(3)]
    inverse = 1.0 / density
    ux = (ex[0] + ex[2] + 4.0 * ex[1]) * inverse
    uy = (dy[0] + dy[2] + 4.0 * dy[1]) * inverse
    uz = (s0[2] - s0[0]) * inverse
    k = [None] * 27
    for r in range(9):
        k[r], k[9 + r], k[18 + r] = forward(g[r], g[9 + r], g[18 + r], ux, t0[r])
    for a in range(3):
        for c in range(3):
            i = 9 * a + c
            k[i], k[i + 3], k[i + 6] = forward(k[i], k[i + 3], k[i + 6], uy, s0[c] if a == 0 else None)
    for i in range(0, 27, 3):
        k[i], k[i + 1], k[i + 2] = forward(k[i], k[i + 1], k[i + 2], uz, density if i == 0 else None)
    for q in range(27):
        k[q] = keep[q] * k[q] if 1 in (q // 9, q // 3 % 3, q % 3) else keep[q] * k[q] + pull[q] * density
    for i in range(0, 27, 3):
        k[i], k[i + 1], k[i + 2] = backward(k[i], k[i + 1], k[i + 2], uz)
    for a in range(3):
        for c in range(3):
            i = 9 * a + c
            k[i], k[i + 3], k[i + 6] = backward(k[i], k[i + 3], k[i + 6], uy)
    for r in range(9):
        k[r], k[9 + r], k[18 + r] = backward(k[r], k[9 + r], k[18 + r], ux)
    return k


def lane(shape):
    return lax.broadcasted_iota(jnp.int32, shape, len(shape) - 1)


def take(values, index):
    return jnp.take_along_axis(values, index, axis=1, mode="promise_in_bounds")


def stretch(values, half=0):
    at = lane(values.shape)
    middle = lax.shift_right_logical(at, 1)
    beside = jnp.clip(middle + 2 * (at & 1) - 1, 0, 63)
    return 0.75 * take(values, middle + 64 * half) + 0.25 * take(values, beside + 64 * half)


def shrink(values):
    at = lane(values.shape)
    even = jnp.minimum(2 * at, 126)
    return (take(values, even) + take(values, even + 1)) * 0.125


def mix(near, far):
    return 0.75 * near + 0.25 * far


def step_kernel(
    given, faces, corners, ends_raw, tall, middle, inner, sums, coarse_stop, table, around,
    fine_next, coarse_next, turned, grid,
    corner_raw, corner_tall, edge_x, edge_y, coarse_out, sems,
):
    inner_copy = pltpu.make_async_copy(inner, fine_next.at[pl.ds(1, 4), pl.ds(1, 4)], sems.at[0])
    inner_copy.start()
    x_copies = [pltpu.make_async_copy(edge_x.at[n], fine_next.at[5 * n], sems.at[1 + n]) for n in range(2)]
    y_copies = [
        pltpu.make_async_copy(edge_y.at[n], fine_next.at[pl.ds(1, 4), 5 * n], sems.at[3 + n]) for n in range(2)
    ]
    coarse_copy = pltpu.make_async_copy(coarse_out, coarse_next, sems.at[5])

    def level(n, rows):
        return around[n, pl.ds(0, rows), :] == 1

    def cell(x, y):
        if x % 5 == 0:
            return edge_x[x // 5, y]
        return edge_y[y // 5, x - 1]

    refined = jnp.max(around[0]) == 1
    for slot in range(4):
        unfold(corner_raw.at[slot], corner_tall.at[slot], corners[slot, pl.ds(0, 16), :])

    def tall_at(i, j, start, count):
        if i % 4 == 0 and j % 4 == 0:
            return corner_tall[i // 4 * 2 + j // 4, pl.ds(start, count), :]
        return tall[i, j, pl.ds(start, count), :]

    @pl.when(refined)
    def _():
        for slot, side in enumerate(FACES):
            dx, dy = side
            pops = face_pops(side)
            edge, inner = 2 + 2 * (dx + dy), 2 + (dx + dy)
            rim = 7 if dx + dy > 0 else 0
            first, count = (pops[0], 9) if dx else (0, 27)
            if dx:
                line = [mix(tall_at(edge, j, first, count), tall_at(inner, j, first, count)) for j in range(5)]
            else:
                line = [mix(tall_at(i, edge, first, count), tall_at(i, inner, first, count)) for i in range(5)]
            cells = []
            for n in range(6):
                cells.append(mix(line[n // 2 + 1], line[n // 2 + 2 * (n % 2)]))
            turn = jnp.swapaxes(jnp.stack(cells), 0, 1)
            fine_there = level(1 + slot, 6)
            for n, q in enumerate(pops):
                values = jnp.where(fine_there, faces[slot, pl.ds(6 * n, 6), :], turn[q - first])
                if dx:
                    turned[q, rim, pl.ds(1, 6), :] = values
                else:
                    turned[q, pl.ds(1, 6), rim, :] = values

        for slot, side in enumerate(CORNERS):
            dx, dy = side
            start = corner_start(side)
            ei, ii, ej, ij = 2 + 2 * dx, 2 + dx, 2 + 2 * dy, 2 + dy
            exploded = mix(
                mix(tall_at(ei, ej, start, 3), tall_at(ii, ej, start, 3)),
                mix(tall_at(ei, ij, start, 3), tall_at(ii, ij, start, 3)),
            )
            value = jnp.where(level(5 + slot, 3), corners[slot, pl.ds(16, 3), :], exploded)
            for c in range(3):
                turned[start + c, 7 if dx > 0 else 0, pl.ds(7 if dy > 0 else 0, 1), :] = value[c : c + 1]

        keep, pull = rates_of(table, 0)

        def advance(load, count):
            at = lane((count, 128))
            still = [load(q, 0, 0) for q in range(27)]
            g = []
            for q in range(27):
                ex, ey, ez = q // 9 - 1, q // 3 % 3 - 1, q % 3 - 1
                source = load(q, ex, ey) if ex or ey else still[q]
                if ez:
                    source = jnp.where(at == (0 if ez > 0 else 127), still[26 - q], pltpu.roll(source, ez % 128, 1))
                g.append(source)
            return jnp.swapaxes(jnp.stack(collide(g, keep, pull)), 0, 1)

        for n in range(2):
            edge_x[n] = advance(lambda q, ex, ey: turned[q, 5 * n + 1 - ex, pl.ds(1 - ey, 6), :], 6)
            x_copies[n].start()
        both = advance(
            lambda q, ex, ey: jnp.concatenate(
                [turned[q, pl.ds(2 - ex, 4), 1 - ey, :], turned[q, pl.ds(2 - ex, 4), 6 - ey, :]], axis=0
            ),
            8,
        )
        for n in range(2):
            edge_y[n] = both[4 * n : 4 * n + 4]
            y_copies[n].start()
        for i in range(3):
            for j in range(3):
                spots = [(x, y) for x in (2 * i, 2 * i + 1) for y in (2 * j, 2 * j + 1)]
                total = sums[i, j]
                for x, y in spots:
                    if x % 5 == 0 or y % 5 == 0:
                        total = total + cell(x, y)
                coarse_out[i, j] = shrink(total)[:, :64]
        coarse_copy.start()

    @pl.when(jnp.logical_not(refined))
    def _():
        for x in range(6):
            line = [mix(tall_at(x // 2 + 1, j, 0, 27), tall_at(x // 2 + 2 * (x % 2), j, 0, 27)) for j in range(5)]
            for y in range(6) if x % 5 == 0 else (0, 5):
                exploded = mix(line[y // 2 + 1], line[y // 2 + 2 * (y % 2)])
                if x % 5 == 0:
                    edge_x[x // 5, y] = exploded
                else:
                    edge_y[y // 5, x - 1] = exploded
            if x % 5 == 0:
                x_copies[x // 5].start()
        for n in range(2):
            y_copies[n].start()

        keep, pull = rates_of(table, 1)
        for n in range(2):
            cells = [ends_raw[n, j, pl.ds(0, 27), :] for j in (1, 2, 3)]
            cells = [corner_raw[2 * n, pl.ds(0, 27), :]] + cells + [corner_raw[2 * n + 1, pl.ds(0, 27), :]]
            cells = jnp.swapaxes(jnp.stack(cells), 0, 1)
            for q in range(27):
                grid[q, pl.ds(20 * n, 5), :] = cells[q]
        g = []
        for q in range(27):
            ex, ey, ez = q // 9 - 1, q // 3 % 3 - 1, q % 3 - 1
            start = 6 - 5 * ex - ey
            source = grid[q, pl.ds(start, 13), :]
            if ez:
                source = pltpu.roll(source, ez % 128, 1)
            if q != 13:
                stop = coarse_stop[ez + 1, pl.ds(start, 13), :]
                source = jnp.where(stop != 0, grid[26 - q, pl.ds(6, 13), :], source)
            g.append(source)
        new = collide(g, keep, pull)
        wall = coarse_stop[1, pl.ds(6, 13), :] != 0
        new = [jnp.where(wall, grid[q, pl.ds(6, 13), :], new[q]) for q in range(27)]
        turn = jnp.swapaxes(jnp.stack(new), 0, 1)
        for i in range(3):
            for j in range(3):
                coarse_out[i, j] = turn[5 * i + j][:, :64]
        coarse_copy.start()

    for copy in [inner_copy, coarse_copy] + x_copies + y_copies:
        copy.wait()


def step(*args):
    vmem = pl.BlockSpec(memory_space=pltpu.VMEM)
    hbm = pl.BlockSpec(memory_space=pltpu.HBM)
    return pl.pallas_call(
        step_kernel,
        out_shape=(
            jax.ShapeDtypeStruct((6, 6, 27, 128), F32),
            jax.ShapeDtypeStruct((3, 3, 27, 64), F32),
            jax.ShapeDtypeStruct((27, 8, 8, 128), F32),
            jax.ShapeDtypeStruct((27, 32, 128), F32),
        ),
        in_specs=[vmem] * 11,
        out_specs=(hbm, hbm, vmem, vmem),
        input_output_aliases={0: 2, 5: 3},
        scratch_shapes=[
            pltpu.VMEM((4, 32, 128), F32),
            pltpu.VMEM((4, 32, 128), F32),
            pltpu.VMEM((2, 6, 27, 128), F32),
            pltpu.VMEM((2, 4, 27, 128), F32),
            pltpu.VMEM((3, 3, 27, 64), F32),
            pltpu.SemaphoreType.DMA((6,)),
        ],
        compiler_params=pltpu.CompilerParams(vmem_limit_bytes=24 * 2**20),
    )(*args)


def solution(mesh):
    n_stream, n_span = mesh.shape["stream"], mesh.shape["span"]

    def local(fine_pops, coarse_pops, obstacle, block_level, relax_rates):
        fine = jnp.transpose(fine_pops, (1, 2, 0, 3))
        coarse = jnp.transpose(coarse_pops, (1, 2, 0, 3))
        ready = exchange(n_stream, n_span, fine, coarse, obstacle, block_level, relax_rates)
        fine_next, coarse_next, *_ = step(*ready)
        return jnp.transpose(fine_next, (2, 0, 1, 3)), jnp.transpose(coarse_next, (2, 0, 1, 3))

    placed = P(None, "stream", "span", None)
    return jax.shard_map(
        local,
        mesh=mesh,
        in_specs=(placed, placed, P("stream", "span", None), P(), P()),
        out_specs=(placed, placed),
        check_vma=False,
    )
```
